128 devices in a mesh: var: 2 (over z_lo), py: 8 (over x, z_hi), pz: 8 (over y, core).
Axes of the slice: x: 4, y: 4, z: 4 (z_hi: 2, z_lo: 2; z = z_hi * 2 + z_lo), core: 2. Of those that a mesh axis runs over, the one named last changes fastest.
Arguments:
- order_field: float32 [12, 256, 256, 256], P('var', 'py', 'pz'), may hold values from 0 to 1
- strains: float32 [24, 6], replicated, may hold values from -2.4 to 2.4
- variant_strain: int32 [24], replicated, may hold values from 0 to 23, each once
Outputs:
- order_next: float32 [12, 256, 256, 256], P('var', 'py', 'pz')
The draws below stay inside these ranges and needn't reach their ends.
Inputs may be any that keep to these rules, and one draw needn't show every extreme that they name: `variant_strain`: each bank row appears once.
All inputs are finite; a program needn't handle non-finite values.
Results may differ from the reference program's by a relative error of at most 0.00026.
Values sent between devices are 32-bit elements; how exact they have to be, the bound alone decides.
No kernel may reach another device: no remote copies, remote signals or barrier semaphores. Data moves between devices by JAX's collectives and lax.ppermute only.
A program may use at most 192 MiB of HBM per device.

```python
import math
import jax
import jax.numpy as jnp
from jax import lax

V = 12
BANK = 24
N = 256
NX = 256


def draw_order_field(key, part):
    key = jax.random.fold_in(key, 7)
    rough_key, offset_key = jax.random.split(key)
    rough_part = jax.random.uniform(rough_key, (V, NX, N, N), jnp.float32)
    offset = jax.random.uniform(offset_key, (V, 1, 1, 1), jnp.float32) * (2.0 * math.pi)
    coords = jnp.arange(N, dtype=jnp.float32) * (2.0 * math.pi / N)
    coords_x = jnp.arange(NX, dtype=jnp.float32) * (2.0 * math.pi / NX)
    along_x = coords_x[:, None, None]
    along_y = coords[None, :, None]
    smooth = jnp.sin(along_x + along_y + offset)
    values = 0.35 * rough_part + 0.325 + 0.3 * smooth
    return jnp.clip(values, 0.0, 1.0)


def gaussian(own_key, dims, deviation, limit, held_as=jnp.bfloat16):
    values = deviation * jax.random.normal(own_key, dims, jnp.float32)
    return jnp.clip(values, min=-limit, max=limit).astype(held_as)


def setup_inputs(seed: int = 0) -> dict:
    key_list = jax.random.split(jax.random.key(seed), 4)
    return {
        "order_field": draw_order_field(jax.random.fold_in(key_list[3], 71), 0),
        "strains": gaussian(key_list[1], (BANK, 6), 0.4, 2.4, jnp.float32),
        "variant_strain": jax.random.permutation(key_list[2], BANK).astype(jnp.int32),
    }


lame_first = 1.5
shear_mod = 1.0
relax_coef = 1.0 / 1.4
grad_coef = 0.5
mobility = 0.2
landau_cubic = 3.0
landau_quartic = 0.5
two_pi = 6.283185307179586
highest = lax.Precision.HIGHEST

def material(strains, variant_strain, variants):
    bank_rows = strains.shape[0]
    picked = variant_strain[:variants]
    one_hot = (picked[:, None] == jnp.arange(bank_rows, dtype=jnp.int32)[None, :]).astype(jnp.float32)
    chosen = jnp.dot(one_hot, strains, precision=highest)
    row_one = jnp.stack([chosen[:, 0], chosen[:, 5], chosen[:, 4]], axis=1)
    row_two = jnp.stack([chosen[:, 5], chosen[:, 1], chosen[:, 3]], axis=1)
    row_three = jnp.stack([chosen[:, 4], chosen[:, 3], chosen[:, 2]], axis=1)
    eigen_strain = jnp.stack([row_one, row_two, row_three], axis=1)
    trace_sum = chosen[:, 0] + chosen[:, 1] + chosen[:, 2]
    stress = lame_first * trace_sum[:, None, None] * jnp.eye(3, dtype=jnp.float32)[None] + 2.0 * shear_mod * eigen_strain
    energy = jnp.einsum('pij,qij->pq', stress, eigen_strain, precision=highest)
    return (stress, energy)

def project_one(stress_one, unit_dir):
    traction = []
    for row_id in range(3):
        total_sum = stress_one[row_id, 0] * unit_dir[0]
        for col_id in range(1, 3):
            total_sum = total_sum + stress_one[row_id, col_id] * unit_dir[col_id]
        traction.append(total_sum)
    normal = unit_dir[0] * traction[0] + unit_dir[1] * traction[1] + unit_dir[2] * traction[2]
    return (traction, normal)

def reference(order_field, strains, variant_strain):
    variants = order_field.shape[0]
    stress, energy = material(strains, variant_strain, variants)
    spectra = jnp.fft.rfftn(order_field, axes=(1, 2, 3))
    indices = jnp.arange(N, dtype=jnp.int32)
    signed = jnp.where(indices >= N // 2, indices - N, indices).astype(jnp.float32)
    x_ids = jnp.arange(NX, dtype=jnp.int32)
    raw_x = jnp.where(x_ids >= NX // 2, x_ids - NX, x_ids).astype(jnp.float32)[:, None, None]
    wave_x = raw_x * (float(N) / float(NX))
    wave_y = signed[None, :, None]
    wave_z = jnp.arange(N // 2 + 1, dtype=jnp.float32)[None, None, :]
    squared_norm = wave_x * wave_x + wave_y * wave_y + wave_z * wave_z
    inverse_norm = lax.rsqrt(jnp.maximum(squared_norm, 1.0))
    unit_dir = (wave_x * inverse_norm, wave_y * inverse_norm, wave_z * inverse_norm)
    keep_mask = jnp.where((raw_x == -(NX // 2)) | (wave_y == -(N // 2)) | (wave_z == N // 2), 0.0, 1.0)
    wave_sq = squared_norm * (two_pi / N) ** 2
    shared = None
    for variant in range(variants):
        traction, normal = project_one(stress[variant], unit_dir)
        terms = [traction[0] * spectra[variant], traction[1] * spectra[variant], traction[2] * spectra[variant], normal * spectra[variant]]
        if shared is None:
            shared = terms
        else:
            shared = [shared[item] + terms[item] for item in range(4)]
    forces = []
    for variant in range(variants):
        traction, normal = project_one(stress[variant], unit_dir)
        mix_term = jnp.tensordot(energy[variant], spectra, axes=1)
        relaxed = traction[0] * shared[0] + traction[1] * shared[1] + traction[2] * shared[2] - relax_coef * normal * shared[3]
        response = keep_mask * (mix_term - relaxed / shear_mod + grad_coef * wave_sq * spectra[variant])
        forces.append(jnp.fft.irfftn(response, s=(NX, N, N), axes=(0, 1, 2)).astype(jnp.float32))
    force_field = jnp.stack(forces, axis=0)
    total_sq = lax.optimization_barrier(jnp.sum(order_field * order_field, axis=0))
    chemical = order_field - landau_cubic * order_field * order_field + landau_quartic * order_field * total_sq[None]
    return order_field - mobility * (chemical + force_field)
```

```python
import functools

import jax
import jax.numpy as jnp
import ml_dtypes
import numpy as np
from jax import lax
from jax.experimental import pallas as pl
from jax.experimental.pallas import tpu as pltpu
from jax.sharding import PartitionSpec as P

lame_first = 1.5
shear_mod = 1.0
relax_coef = 1.0 / 1.4
grad_coef = 0.5
mobility = 0.2
landau_cubic = 3.0
landau_quartic = 0.5
two_pi = 6.283185307179586
highest = lax.Precision.HIGHEST
every = ("var", "py", "pz")
vmem_bytes = 48 * 1024 * 1024

forward_chunks = ((0, 1), (2,))
backward_chunks = ((0,), (1, 2))


def split_table(table):
    high = table.astype(ml_dtypes.bfloat16)
    low = (table - high.astype(np.float64)).astype(ml_dtypes.bfloat16)
    return high, low


def left_table(table):
    high, low = split_table(table)
    return np.concatenate([high, low, high], axis=1)


def right_table(table):
    high, low = split_table(table)
    return np.concatenate([high, high, low], axis=0)


@functools.cache
def dft_tables(length):
    half = length // 2
    ids = np.arange(length)
    angles = (ids[:, None] * ids[None, :] % length) * (2.0 * np.pi / length)
    cos, sin = np.cos(angles), np.sin(angles)
    z_fwd = left_table(np.concatenate([cos[:half], -sin[:half]], axis=0))
    weight = np.where(np.arange(half) == 0, 1.0, 2.0)[:, None]
    z_back = right_table(np.concatenate([cos[:half] * weight, -sin[:half] * weight], axis=0))
    y_both = left_table(np.concatenate([cos, sin], axis=0))
    blocks = 8
    width = length // blocks
    fwd = np.empty((2, length, 2, length))
    fwd[0, :, 0], fwd[0, :, 1] = cos, -sin
    fwd[1, :, 0], fwd[1, :, 1] = sin, cos
    fwd = fwd.reshape(2, blocks // 2, 2, width, 2 * length).transpose(1, 0, 2, 3, 4)
    x_fwd = right_table(fwd.reshape(2 * length, 2 * length))
    back = np.empty((2, length, 2, length))
    back[0, :, 0], back[0, :, 1] = cos, sin
    back[1, :, 0], back[1, :, 1] = -sin, cos
    back = back.reshape(2 * length, 2, blocks // 2, 2, width).transpose(0, 2, 1, 3, 4)
    x_back = right_table(back.reshape(2 * length, 2 * length))
    return z_fwd, z_back, y_both, x_fwd, x_back


def split_value(value):
    high = value.astype(jnp.bfloat16)
    low = (value - high.astype(jnp.float32)).astype(jnp.bfloat16)
    return high, low


def as_left(value):
    high, low = split_value(value)
    return jnp.concatenate([high, low, high], axis=1)


def as_right(value):
    high, low = split_value(value)
    return jnp.concatenate([high, high, low], axis=0)


def matmul(left, right):
    return lax.dot_general(
        left, right, (((1,), (0,)), ((), ())), preferred_element_type=jnp.float32
    )


def matmul_tr(left, right):
    return lax.dot_general(
        left, right, (((1,), (1,)), ((), ())), preferred_element_type=jnp.float32
    )


def lane_ids(rows):
    return lax.broadcasted_iota(jnp.int32, (rows, 128), 1)


def z_forward(first_ref, second_ref, table_ref, *refs):
    out_ref, sq_ref = refs[-2:]
    group = pl.program_id(1)
    for side, ref in enumerate((first_ref, second_ref)):
        phi = ref[...]
        squares = phi[0] * phi[0] + phi[1] * phi[1]
        lanes = slice(side * 128, side * 128 + 128)
        before = refs[0][:, :, lanes] if len(refs) == 3 else 0.0
        sq_ref[:, :, lanes] = jnp.where(group > 0, sq_ref[:, :, lanes], before) + squares

    row_refs = [first_ref.reshape(512, 128), second_ref.reshape(512, 128)]
    flat_ref = out_ref.reshape(1024, 128)
    low_half = lane_ids(128) < 64
    for batch in range(2):
        block = jnp.concatenate(
            [
                jnp.concatenate(
                    [ref[pl.ds(batch * 4 + y, 64, stride=8), :] for ref in row_refs], axis=1
                )
                for y in range(4)
            ],
            axis=0,
        )
        high, low = split_value(block)
        spectrum = matmul_tr(table_ref[...], jnp.concatenate([high, high, low], axis=1))
        for pair in range(2):
            real = spectrum[:128, pair * 128 : pair * 128 + 128]
            imag = spectrum[128:, pair * 128 : pair * 128 + 128]
            even = jnp.where(low_half, real, pltpu.roll(imag, 64, 1))
            odd = jnp.where(low_half, pltpu.roll(real, 64, 1), imag)
            y = batch * 4 + pair * 2
            flat_ref[pl.ds(y, 128, stride=8), :] = even
            flat_ref[pl.ds(y + 1, 128, stride=8), :] = odd


def xy_forward(in_ref, y_ref, x_ref, out_ref, left_ref):
    lanes = lane_ids(256)
    low_half = lanes < 64
    even_lane = (lanes // 32) % 2 == 0
    for pair in range(4):
        first = in_ref[pair * 16 : pair * 16 + 8].reshape(256, 128)
        second = in_ref[pair * 16 + 8 : pair * 16 + 16].reshape(256, 128)
        both = matmul(y_ref[...], as_right(jnp.concatenate([first, second], axis=1)))
        done = []
        for side in range(2):
            cos_part = both[:256, side * 128 : side * 128 + 128]
            sin_part = pltpu.roll(both[256:, side * 128 : side * 128 + 128], 64, 1)
            done.append(cos_part + jnp.where(low_half, sin_part, -sin_part))
        zero = jnp.where(even_lane, done[0], pltpu.roll(done[1], 32, 1))
        one = jnp.where(even_lane, pltpu.roll(done[0], 96, 1), done[1])
        for v, value in enumerate((zero, one)):
            high, low = split_value(value)
            rows = slice(v * 256, v * 256 + 256)
            left_ref[rows, pair * 128 : pair * 128 + 128] = high
            left_ref[rows, 512 + pair * 128 : 512 + pair * 128 + 128] = low
            left_ref[rows, 1024 + pair * 128 : 1024 + pair * 128 + 128] = high
    for v in range(2):
        out_ref[v] = matmul(left_ref[v * 256 : v * 256 + 256, :], x_ref[...])


def xy_back(in_ref, x_ref, y_ref, out_ref, mid_ref):
    lanes = lane_ids(256)
    low_half = lanes < 64
    even_lane = (lanes // 32) % 2 == 0
    for v in range(2):
        mid_ref[v] = matmul(as_left(in_ref[v]), x_ref[...])
    for pair in range(4):
        zero = mid_ref[0, :, pair * 128 : pair * 128 + 128]
        one = mid_ref[1, :, pair * 128 : pair * 128 + 128]
        first = jnp.where(even_lane, zero, pltpu.roll(one, 32, 1))
        second = jnp.where(even_lane, pltpu.roll(zero, 96, 1), one)
        both = matmul(y_ref[...], as_right(jnp.concatenate([first, second], axis=1)))
        for side in range(2):
            cos_part = both[:256, side * 128 : side * 128 + 128]
            sin_part = pltpu.roll(both[256:, side * 128 : side * 128 + 128], 64, 1)
            value = cos_part + jnp.where(low_half, -sin_part, sin_part)
            start = pair * 16 + side * 8
            out_ref[start : start + 8] = value.reshape(8, 32, 128)


def mix_kernel(n_in, n_out, places_in, places_out, rows, length, coef_ref, *refs):
    ins, outs = refs[:n_in], refs[n_in : n_in + n_out]
    half = length // 2
    wave_z = coef_ref[12, 0]
    base = pl.program_id(0) * rows
    volume = 1.0 / float(length * length * length)

    def tile(index, carry):
        row = pl.multiple_of(index * 8, 8)
        ky = lax.broadcasted_iota(jnp.int32, (8, length), 0) + (base + row)
        kx = lax.broadcasted_iota(jnp.int32, (8, length), 1)
        wy = jnp.where(ky >= half, ky - length, ky).astype(jnp.float32)
        wx = jnp.where(kx >= half, kx - length, kx).astype(jnp.float32)
        wz = jnp.full((8, length), wave_z, jnp.float32)
        squared = wx * wx + wy * wy + wz * wz
        inverse = 1.0 / jnp.maximum(squared, 1.0)
        keep = jnp.where((ky == half) | (kx == half), 0.0, volume)
        grad = keep * squared * (grad_coef * (two_pi / length) ** 2)

        def field(p):
            place, group, var, v = places_in[p]
            return ins[place][group, var, v, pl.ds(row, 8), :]

        strains = []
        for q in range(12):
            value = field(q)
            for m in range(6):
                term = coef_ref[q, m] * value
                if q == 0:
                    strains.append(term)
                else:
                    strains[m] = strains[m] + term
        drives = []
        for part in range(2):
            strain = [total[:, part * length : (part + 1) * length] for total in strains]
            trace = lame_first * (strain[0] + strain[1] + strain[2])
            s11 = trace + 2.0 * shear_mod * strain[0]
            s22 = trace + 2.0 * shear_mod * strain[1]
            s33 = trace + 2.0 * shear_mod * strain[2]
            s23 = 2.0 * shear_mod * strain[3]
            s13 = 2.0 * shear_mod * strain[4]
            s12 = 2.0 * shear_mod * strain[5]
            t1 = (s11 * wx + s12 * wy + s13 * wz) * inverse
            t2 = (s12 * wx + s22 * wy + s23 * wz) * inverse
            t3 = (s13 * wx + s23 * wy + s33 * wz) * inverse
            normal = (wx * t1 + wy * t2 + wz * t3) * (relax_coef * inverse)
            u1 = t1 - normal * wx
            u2 = t2 - normal * wy
            u3 = t3 - normal * wz
            drives.append(
                [
                    keep * (strain[0] - wx * u1),
                    keep * (strain[1] - wy * u2),
                    keep * (strain[2] - wz * u3),
                    keep * (2.0 * strain[3] - (wy * u3 + wz * u2)),
                    keep * (2.0 * strain[4] - (wx * u3 + wz * u1)),
                    keep * (2.0 * strain[5] - (wx * u2 + wy * u1)),
                ]
            )
        drive = [jnp.concatenate([drives[0][m], drives[1][m]], axis=1) for m in range(6)]
        both_grad = jnp.concatenate([grad, grad], axis=1)
        for p in range(12):
            total = both_grad * field(p)
            for m in range(6):
                total = total + coef_ref[p, 6 + m] * drive[m]
            place, group, var, v = places_out[p]
            outs[place][group, var, v, pl.ds(row, 8), :] = total
        return carry

    lax.fori_loop(0, rows // 8, tile, 0)


def z_back(spec_ref, phi_ref, own_ref, partner_ref, table_ref, *rest):
    out_ref, force_ref = rest[-2:]
    flat_ref = spec_ref.reshape(1024, 128)
    row_refs = [force_ref.at[side].reshape(512, 128) for side in range(2)]
    for batch in range(2):
        lefts = []
        for y in range(4):
            turned = flat_ref[pl.ds(batch * 4 + y, 128, stride=8), :].T
            lefts.append(jnp.concatenate([turned[:64], turned[64:]], axis=1))
        force = matmul(as_left(jnp.concatenate(lefts, axis=0)), table_ref[...])
        for y in range(4):
            rows = pl.ds(batch * 4 + y, 64, stride=8)
            for side, ref in enumerate(row_refs):
                lanes = slice(side * 128, side * 128 + 128)
                ref[rows, :] = force[y * 64 : y * 64 + 64, lanes]
    for side in range(2):
        lanes = slice(side * 128, side * 128 + 128)
        total_sq = own_ref[:, :, lanes] + partner_ref[:, :, lanes]
        for v in range(2):
            phi = phi_ref[v, :, :, lanes]
            chemical = phi - landau_cubic * phi * phi + landau_quartic * phi * total_sq
            out_ref[v, :, :, lanes] = phi - mobility * (chemical + force_ref[side, v])


def params(count):
    return pltpu.CompilerParams(
        dimension_semantics=("arbitrary",) * count, vmem_limit_bytes=vmem_bytes
    )


def cost(flops, moved):
    return pl.CostEstimate(flops=int(flops), bytes_accessed=int(moved), transcendentals=0)


def whole(array):
    return pl.BlockSpec(array.shape, lambda *ids: (0,) * array.ndim)


group_bytes = 2 * 32 * 32 * 256 * 4


def call_z_forward(phi, table, chunk, squares):
    count, start = len(chunk), chunk[0]
    earlier = [] if squares is None else [squares]
    return pl.pallas_call(
        z_forward,
        grid=(4, count),
        in_specs=[
            pl.BlockSpec((2, 32, 8, 128), lambda j, g: (g + start, 0, j, 0)),
            pl.BlockSpec((2, 32, 8, 128), lambda j, g: (g + start, 0, j, 1)),
            whole(table),
        ]
        + [pl.BlockSpec((32, 8, 256), lambda j, g: (0, j, 0)) for _ in earlier],
        out_specs=[
            pl.BlockSpec((128, 8, 128), lambda j, g: (0, g * 4 + j, 0)),
            pl.BlockSpec((32, 8, 256), lambda j, g: (0, j, 0)),
        ],
        out_shape=[
            jax.ShapeDtypeStruct((128, 32 * count, 128), jnp.float32),
            jax.ShapeDtypeStruct((32, 32, 256), jnp.float32),
        ],
        compiler_params=params(2),
        cost_estimate=cost(count * 0.81e9, count * 2 * group_bytes),
        name="z_forward",
    )(phi, phi, table, *earlier)


def call_xy_forward(spec, y_table, x_table, chunk):
    count = len(chunk)
    return pl.pallas_call(
        xy_forward,
        grid=(count, 2),
        in_specs=[
            pl.BlockSpec((64, 32, 128), lambda g, a: (a, g, 0)),
            whole(y_table),
            whole(x_table),
        ],
        out_specs=pl.BlockSpec((None, None, 2, 256, 512), lambda g, a: (g, a, 0, 0, 0)),
        out_shape=jax.ShapeDtypeStruct((count, 2, 2, 256, 512), jnp.float32),
        scratch_shapes=[pltpu.VMEM((512, 1536), jnp.bfloat16)],
        compiler_params=params(2),
        cost_estimate=cost(count * 3.2e9, count * 2 * group_bytes),
        name="xy_forward",
    )(spec, y_table, x_table)


def call_mix(coefs, specs, length):
    rows = 32

    def places(chunks):
        where = {g: (c, i) for c, chunk in enumerate(chunks) for i, g in enumerate(chunk)}
        return tuple(where[p % 6 // 2] + (p // 6, p % 2) for p in range(12))

    def spec_of(chunk):
        return pl.BlockSpec((len(chunk), 2, 2, rows, 512), lambda j: (0, 0, 0, j, 0))

    body = functools.partial(
        mix_kernel,
        len(forward_chunks),
        len(backward_chunks),
        places(forward_chunks),
        places(backward_chunks),
        rows,
        length,
    )
    return pl.pallas_call(
        body,
        grid=(length // rows,),
        in_specs=[pl.BlockSpec(memory_space=pltpu.SMEM)] + [spec_of(c) for c in forward_chunks],
        out_specs=[spec_of(c) for c in backward_chunks],
        out_shape=[
            jax.ShapeDtypeStruct((len(c), 2, 2, 256, 512), jnp.float32) for c in backward_chunks
        ],
        compiler_params=params(1),
        cost_estimate=cost(50e6, 6 * group_bytes),
        name="mixing",
    )(coefs, *specs)


def call_xy_back(resp, x_table, y_table, chunk):
    count = len(chunk)
    return pl.pallas_call(
        xy_back,
        grid=(count, 2),
        in_specs=[
            pl.BlockSpec((None, None, 2, 256, 512), lambda g, a: (g, a, 0, 0, 0)),
            whole(x_table),
            whole(y_table),
        ],
        out_specs=pl.BlockSpec((64, 32, 128), lambda g, a: (a, g, 0)),
        out_shape=jax.ShapeDtypeStruct((128, 32 * count, 128), jnp.float32),
        scratch_shapes=[pltpu.VMEM((2, 256, 512), jnp.float32)],
        compiler_params=params(2),
        cost_estimate=cost(count * 3.2e9, count * 2 * group_bytes),
        name="xy_back",
    )(resp, x_table, y_table)


def call_z_back(spec, phi, own, partner, table, chunk, partial):
    count, start = len(chunk), chunk[0]
    operands = [spec, phi, own, partner, table]
    specs = [
        pl.BlockSpec((128, 8, 128), lambda j, g: (0, g * 4 + j, 0)),
        pl.BlockSpec((2, 32, 8, 256), lambda j, g: (g + start, 0, j, 0)),
        pl.BlockSpec((32, 8, 256), lambda j, g: (0, j, 0)),
        pl.BlockSpec((32, 8, 256), lambda j, g: (0, j, 0)),
        whole(table),
    ]
    aliases = {}
    if partial is not None:
        operands.append(partial)
        specs.append(pl.BlockSpec(memory_space=pl.ANY))
        aliases = {5: 0}
    return pl.pallas_call(
        z_back,
        grid=(4, count),
        in_specs=specs,
        out_specs=pl.BlockSpec((2, 32, 8, 256), lambda j, g: (g + start, 0, j, 0)),
        out_shape=jax.ShapeDtypeStruct(phi.shape, jnp.float32),
        input_output_aliases=aliases,
        scratch_shapes=[pltpu.VMEM((2, 2, 32, 8, 128), jnp.float32)],
        compiler_params=params(2),
        cost_estimate=cost(count * 0.81e9, count * 3 * group_bytes),
        name="z_back",
    )(*operands)


def exchange(block):
    return lax.all_to_all(block, every, split_axis=0, concat_axis=0, tiled=True)


def after(block, earlier):
    return lax.optimization_barrier((block, earlier[-1]))[0] if earlier else block


def coefficients(strains, variant_strain, variants):
    bank_rows = strains.shape[0]
    picked = variant_strain[:variants]
    one_hot = (picked[:, None] == jnp.arange(bank_rows, dtype=jnp.int32)[None, :]).astype(
        jnp.float32
    )
    chosen = jnp.dot(one_hot, strains, precision=highest)
    trace = lame_first * (chosen[:, 0] + chosen[:, 1] + chosen[:, 2])
    diagonal = jnp.asarray([1.0, 1.0, 1.0, 0.0, 0.0, 0.0], jnp.float32)
    stress = trace[:, None] * diagonal[None, :] + 2.0 * shear_mod * chosen
    plane = lax.axis_index(every).astype(jnp.float32)
    last = jnp.full((1, 12), plane, jnp.float32)
    return jnp.concatenate([jnp.concatenate([chosen, stress], axis=1), last], axis=0)


def shards(order_field, strains, variant_strain):
    length = order_field.shape[3]
    z_fwd, z_inv, y_both, x_fwd, x_inv = [jnp.asarray(t) for t in dft_tables(length)]
    coefs = coefficients(strains, variant_strain, 12)
    squares = None
    arrived = []
    for chunk in forward_chunks:
        sent, squares = call_z_forward(order_field, z_fwd, chunk, squares)
        arrived.append(exchange(after(sent, arrived)))
    specs = [
        call_xy_forward(block, y_both, x_fwd, chunk)
        for block, chunk in zip(arrived[:-1], forward_chunks)
    ]
    squares, arrived[-1], *specs = lax.optimization_barrier((squares, arrived[-1], *specs))
    partner = lax.ppermute(squares, "var", [(0, 1), (1, 0)])
    specs.append(call_xy_forward(arrived[-1], y_both, x_fwd, forward_chunks[-1]))
    resps = call_mix(coefs, specs, length)
    sends = []
    for resp, chunk in zip(resps, backward_chunks):
        sends.append(call_xy_back(resp, x_inv, y_both, chunk))
    sends[0], partner = lax.optimization_barrier((sends[0], partner))
    result = None
    returned = []
    for send, chunk in zip(sends, backward_chunks):
        returned.append(exchange(after(send, returned)))
        block = returned[-1]
        result = call_z_back(
            block, order_field, squares, partner, z_inv, chunk, result
        )
    return result


def solution(mesh):
    placed = (P("var", "py", "pz", None), P(), P())
    return jax.shard_map(
        shards, mesh=mesh, in_specs=placed, out_specs=P("var", "py", "pz", None), check_vma=False
    )
```

```python
import functools

import jax
import jax.numpy as jnp
import ml_dtypes
import numpy as np
from jax import lax
from jax.experimental import pallas as pl
from jax.experimental.pallas import tpu as pltpu
from jax.sharding import PartitionSpec as P

lame_first = 1.5
shear_mod = 1.0
relax_coef = 1.0 / 1.4
grad_coef = 0.5
mobility = 0.2
landau_cubic = 3.0
landau_quartic = 0.5
two_pi = 6.283185307179586
highest = lax.Precision.HIGHEST
every = ("var", "py", "pz")
vmem_bytes = 48 * 1024 * 1024

groups = 3


def split_table(table):
    high = table.astype(ml_dtypes.bfloat16)
    low = (table - high.astype(np.float64)).astype(ml_dtypes.bfloat16)
    return high, low


def left_table(table):
    return np.concatenate(split_table(table), axis=1)


def right_table(table):
    return np.concatenate(split_table(table), axis=0)


def complex_blocks(angles, sign):
    cos, sin = np.cos(angles), sign * np.sin(angles)
    table = np.empty((2, angles.shape[0], 2, angles.shape[1]))
    table[0, :, 0], table[0, :, 1] = cos, sin
    table[1, :, 0], table[1, :, 1] = -sin, cos
    return table


@functools.cache
def dft_tables(length):
    half = length // 2
    ids = np.arange(length)
    unit = 2.0 * np.pi / length
    angles = (ids[:, None] * ids[None, :] % length) * unit
    cos, sin = np.cos(angles), np.sin(angles)
    z_fwd = left_table(np.concatenate([cos[:half], -sin[:half]], axis=0))
    weight = np.where(np.arange(half) == 0, 1.0, 2.0)[:, None]
    z_back = right_table(np.concatenate([cos[:half] * weight, -sin[:half] * weight], axis=0))
    low = np.arange(half)
    blocks = 8
    width = length // blocks
    y_fwd, y_back, x_fwd, x_back = [], [], [], []
    for parity in range(2):
        y_ids = 2 * low + parity
        fwd = complex_blocks((y_ids[:, None] * low[None, :] % length) * unit, -1.0)
        fwd = fwd.reshape(2, blocks, width // 2, length)
        y_fwd.append(left_table(fwd.transpose(3, 1, 0, 2).reshape(length, length)))
        back = complex_blocks((low[:, None] * y_ids[None, :] % length) * unit, 1.0)
        back = back.reshape(length, 2, blocks, width // 2)
        y_back.append(left_table(back.transpose(2, 1, 3, 0).reshape(length, length)))
        x_ids = low.reshape(2, 2, width).transpose(1, 0, 2).reshape(half)
        k_ids = 2 * low + parity
        fwd = complex_blocks((x_ids[:, None] * k_ids[None, :] % length) * unit, -1.0)
        x_fwd.append(right_table(fwd.reshape(length, length)))
        back = complex_blocks((k_ids[:, None] * x_ids[None, :] % length) * unit, 1.0)
        x_back.append(right_table(back.reshape(length, length)))
    return z_fwd, z_back, np.stack(y_fwd), np.stack(y_back), np.stack(x_fwd), np.stack(x_back)


def split_value(value):
    high = value.astype(jnp.bfloat16)
    low = (value - high.astype(jnp.float32)).astype(jnp.bfloat16)
    return high, low


def as_left(value):
    high, low = split_value(value)
    return jnp.concatenate([high, low, high], axis=1)


def as_right_tr(value):
    high, low = split_value(value)
    return jnp.concatenate([high, high, low], axis=1)


def as_right(value):
    high, low = split_value(value)
    return jnp.concatenate([high, high, low], axis=0)


def left_rows(table):
    width = table.shape[1] // 2
    return jnp.concatenate([table, table[:, :width]], axis=1)


def right_rows(table):
    depth = table.shape[0] // 2
    return jnp.concatenate([table[:depth], table], axis=0)


def matmul(left, right):
    return lax.dot_general(
        left, right, (((1,), (0,)), ((), ())), preferred_element_type=jnp.float32
    )


def matmul_tr(left, right):
    return lax.dot_general(
        left, right, (((1,), (1,)), ((), ())), preferred_element_type=jnp.float32
    )


def lane_ids(rows):
    return lax.broadcasted_iota(jnp.int32, (rows, 128), 1)


def z_forward(first_ref, second_ref, table_ref, out_ref, sq_ref):
    group = pl.program_id(1)
    for side, ref in enumerate((first_ref, second_ref)):
        phi = ref[...]
        squares = phi[0] * phi[0] + phi[1] * phi[1]
        lanes = slice(side * 128, side * 128 + 128)
        sq_ref[:, :, lanes] = jnp.where(group > 0, sq_ref[:, :, lanes], 0.0) + squares

    row_refs = [first_ref.reshape(1024, 128), second_ref.reshape(1024, 128)]
    flat_ref = out_ref.reshape(2048, 128)
    for batch in range(4):
        block = jnp.concatenate(
            [
                jnp.concatenate(
                    [ref[pl.ds(batch * 4 + y, 64, stride=16), :] for ref in row_refs], axis=1
                )
                for y in range(4)
            ],
            axis=0,
        )
        spectrum = matmul_tr(left_rows(table_ref[...]), as_right_tr(block))
        for pair in range(2):
            for part in range(2):
                rows = pl.ds(part * 8 + batch * 2 + pair, 128, stride=16)
                flat_ref[rows, :] = spectrum[
                    part * 128 : part * 128 + 128, pair * 128 : pair * 128 + 128
                ]


def transform_there(in_ref, y_ref, x_ref, out_ref, left_ref):
    lanes = lane_ids(256)
    low_half = lanes < 64
    first_bit = lane_ids(128) // 32 % 2 == 0
    halves = []
    for pp in range(2):
        evens, odds = [], []
        for place in (pp, pp + 2):
            first = in_ref[place * 16 : place * 16 + 8].reshape(256, 128)
            second = in_ref[place * 16 + 8 : place * 16 + 16].reshape(256, 128)
            evens.append(jnp.where(low_half, first, pltpu.roll(second, 64, 1)))
            odds.append(jnp.where(low_half, pltpu.roll(first, 64, 1), second))
        even = matmul(left_rows(y_ref[0]), as_right(jnp.concatenate(evens, axis=1)))
        odd = matmul(left_rows(y_ref[1]), as_right(jnp.concatenate(odds, axis=1)))
        low, high = even + odd, even - odd
        halves.append(
            [
                [side[:, :128] + side[:, 128:], side[:, :128] - side[:, 128:]]
                for side in (low, high)
            ]
        )
    for parity in range(2):
        for side in range(2):
            for part in range(2):
                rows = slice(part * 128, part * 128 + 128)
                zero = halves[0][side][parity][rows]
                one = halves[1][side][parity][rows]
                values = (
                    jnp.where(first_bit, zero, pltpu.roll(one, 32, 1)),
                    jnp.where(first_bit, pltpu.roll(zero, 96, 1), one),
                )
                for v, value in enumerate(values):
                    high, low = split_value(value)
                    start = v * 256 + side * 128
                    for third, piece in enumerate((high, low, high)):
                        column = third * 256 + part * 128
                        left_ref[parity, start : start + 128, column : column + 128] = piece
    for parity in range(2):
        product = matmul(left_ref[parity], right_rows(x_ref[parity]))
        for v in range(2):
            out_ref[v, :, parity * 256 : parity * 256 + 256] = product[v * 256 : v * 256 + 256]


def transform_back(in_ref, x_ref, y_ref, out_ref):
    lanes = lane_ids(256)
    low_half = lanes < 64
    first_bit = lanes // 32 % 2 == 0
    products = []
    for parity in range(2):
        columns = slice(parity * 256, parity * 256 + 256)
        block = jnp.concatenate([in_ref[0, :, columns], in_ref[1, :, columns]], axis=0)
        products.append(matmul(as_left(block), right_rows(x_ref[parity])))
    for side in range(2):
        field = products[0] + products[1] if side == 0 else products[0] - products[1]
        evens, odds = ([], []), ([], [])
        for part in range(2):
            zero = field[:256, part * 128 : part * 128 + 128]
            one = field[256:, part * 128 : part * 128 + 128]
            merged = (
                jnp.where(first_bit, zero, pltpu.roll(one, 32, 1)),
                jnp.where(first_bit, pltpu.roll(zero, 96, 1), one),
            )
            for pp in range(2):
                evens[pp].append(merged[pp][:128] + merged[pp][128:])
                odds[pp].append(merged[pp][:128] - merged[pp][128:])
        results = []
        for parity, pieces in enumerate((evens, odds)):
            right = jnp.concatenate([jnp.concatenate(p, axis=0) for p in pieces], axis=1)
            results.append(matmul(left_rows(y_ref[parity]), as_right(right)))
        for pp in range(2):
            even = results[0][:, pp * 128 : pp * 128 + 128]
            odd = results[1][:, pp * 128 : pp * 128 + 128]
            start = (side * 2 + pp) * 16
            first = jnp.where(low_half, even, pltpu.roll(odd, 64, 1))
            second = jnp.where(low_half, pltpu.roll(even, 64, 1), odd)
            out_ref[start : start + 8] = first.reshape(8, 2, 16, 128)
            out_ref[start + 8 : start + 16] = second.reshape(8, 2, 16, 128)


def waves(row, wave_z, length):
    half = length // 2
    ky = lax.broadcasted_iota(jnp.int32, (8, length), 0) + row
    column = lax.broadcasted_iota(jnp.int32, (8, length), 1)
    kx = column % half * 2 + column // half
    wy = jnp.where(ky >= half, ky - length, ky).astype(jnp.float32)
    wx = jnp.where(kx >= half, kx - length, kx).astype(jnp.float32)
    wz = jnp.full((8, length), wave_z, jnp.float32)
    squared = wx * wx + wy * wy + wz * wz
    volume = 1.0 / float(length * length * length)
    keep = jnp.where((ky == half) | (kx == half), 0.0, volume)
    grad = keep * squared * (grad_coef * (two_pi / length) ** 2)
    return wx, wy, wz, squared, keep, join(grad, grad)


def pick(value, part):
    half = value.shape[1] // 4
    return jnp.concatenate(
        [value[:, c * half : (c + 1) * half] for c in (part, part + 2)], axis=1
    )


def join(real, imag):
    half = real.shape[1] // 2
    pieces = [real[:, :half], imag[:, :half], real[:, half:], imag[:, half:]]
    return jnp.concatenate(pieces, axis=1)


def driving(strain, wx, wy, wz, squared, keep):
    inverse = 1.0 / jnp.maximum(squared, 1.0)
    trace = lame_first * (strain[0] + strain[1] + strain[2])
    s11 = trace + 2.0 * shear_mod * strain[0]
    s22 = trace + 2.0 * shear_mod * strain[1]
    s33 = trace + 2.0 * shear_mod * strain[2]
    s23 = 2.0 * shear_mod * strain[3]
    s13 = 2.0 * shear_mod * strain[4]
    s12 = 2.0 * shear_mod * strain[5]
    t1 = (s11 * wx + s12 * wy + s13 * wz) * inverse
    t2 = (s12 * wx + s22 * wy + s23 * wz) * inverse
    t3 = (s13 * wx + s23 * wy + s33 * wz) * inverse
    normal = (wx * t1 + wy * t2 + wz * t3) * (relax_coef * inverse)
    u1 = t1 - normal * wx
    u2 = t2 - normal * wy
    u3 = t3 - normal * wz
    return [
        keep * (strain[0] - wx * u1),
        keep * (strain[1] - wy * u2),
        keep * (strain[2] - wz * u3),
        keep * (2.0 * strain[3] - (wy * u3 + wz * u2)),
        keep * (2.0 * strain[4] - (wx * u3 + wz * u1)),
        keep * (2.0 * strain[5] - (wx * u2 + wy * u1)),
    ]


def middle(coef_ref, in_hbm, yf_hbm, xf_hbm, xb_hbm, yb_hbm, out_hbm, *scratch):
    in_ref, yf_ref, xf_ref, xb_ref, yb_ref, field_ref, left_ref, out_ref, sems = scratch
    length = field_ref.shape[1]
    wave_z = coef_ref[12, 0]
    steps = groups * 2

    def part_of(ref, step):
        return ref.at[
            pl.ds(pl.multiple_of(step % 2 * 64, 64), 64),
            pl.ds(pl.multiple_of(step // 2 * 2, 2), 2),
        ]

    def arrival(step):
        slot = step % 2
        return pltpu.make_async_copy(part_of(in_hbm, step), in_ref.at[slot], sems.at[slot])

    def departure(step):
        slot = step % 2
        return pltpu.make_async_copy(out_ref.at[slot], part_of(out_hbm, step), sems.at[2 + slot])

    moves = [(yf_hbm, yf_ref), (xf_hbm, xf_ref), (xb_hbm, xb_ref), (yb_hbm, yb_ref)]
    copies = [
        pltpu.make_async_copy(source, target, sems.at[4 + number])
        for number, (source, target) in enumerate(moves)
    ]
    copies[0].start()
    arrival(0).start()
    for copy in copies[1:]:
        copy.start()
    copies[0].wait()
    copies[1].wait()

    def there(step, carry):
        @pl.when(step + 1 < steps)
        def _():
            arrival(step + 1).start()

        arrival(step).wait()
        transform_there(
            in_ref.at[step % 2], yf_ref, xf_ref, field_ref.at[pl.ds(step * 2, 2)], left_ref
        )
        return carry

    lax.fori_loop(0, steps, there, 0)
    places = [(p % 6 // 2 * 2 + p // 6) * 2 + p % 2 for p in range(12)]

    def tile(step, carry):
        row = pl.multiple_of(step * 8, 8)
        rows = pl.ds(row, 8)
        wx, wy, wz, squared, keep, grad = waves(row, wave_z, length)
        strains = None
        for q, place in enumerate(places):
            value = field_ref[place, rows, :]
            terms = [coef_ref[q, m] * value for m in range(6)]
            strains = terms if q == 0 else [total + term for total, term in zip(strains, terms)]
        parts = [
            driving([pick(total, part) for total in strains], wx, wy, wz, squared, keep)
            for part in range(2)
        ]
        drive = [join(parts[0][m], parts[1][m]) for m in range(6)]
        for p, place in enumerate(places):
            total = grad * field_ref[place, rows, :]
            for m in range(6):
                total = total + coef_ref[p, 6 + m] * drive[m]
            field_ref[place, rows, :] = total
        return carry

    lax.fori_loop(0, length // 8, tile, 0)
    copies[2].wait()
    copies[3].wait()

    def back(step, carry):
        @pl.when(step >= 2)
        def _():
            departure(step - 2).wait()

        transform_back(field_ref.at[pl.ds(step * 2, 2)], xb_ref, yb_ref, out_ref.at[step % 2])
        departure(step).start()
        return carry

    lax.fori_loop(0, steps, back, 0)
    departure(steps - 2).wait()
    departure(steps - 1).wait()


def z_back(spec_ref, phi_ref, own_ref, partner_ref, table_ref, out_ref, force_ref):
    flat_ref = spec_ref.reshape(2048, 128)
    row_refs = [force_ref.at[side].reshape(1024, 128) for side in range(2)]
    for batch in range(4):
        lefts = []
        for pair in range(2):
            turned = [
                flat_ref[pl.ds(part * 8 + batch * 2 + pair, 128, stride=16), :].T
                for part in range(2)
            ]
            lefts.append(jnp.concatenate(turned, axis=1))
        force = matmul(as_left(jnp.concatenate(lefts, axis=0)), right_rows(table_ref[...]))
        for y in range(4):
            rows = pl.ds(batch * 4 + y, 64, stride=16)
            for side, ref in enumerate(row_refs):
                lanes = slice(side * 128, side * 128 + 128)
                ref[rows, :] = force[y * 64 : y * 64 + 64, lanes]
    for side in range(2):
        lanes = slice(side * 128, side * 128 + 128)
        total_sq = own_ref[:, :, lanes] + partner_ref[:, :, lanes]
        for v in range(2):
            phi = phi_ref[v, :, :, lanes]
            chemical = phi - landau_cubic * phi * phi + landau_quartic * phi * total_sq
            out_ref[v, :, :, lanes] = phi - mobility * (chemical + force_ref[side, v])


def params(count):
    return pltpu.CompilerParams(
        dimension_semantics=("arbitrary",) * count, vmem_limit_bytes=vmem_bytes
    )


def cost(flops, moved):
    return pl.CostEstimate(flops=int(flops), bytes_accessed=int(moved), transcendentals=0)


def hbm(shape):
    return pltpu.HBM(shape, jnp.float32)


def in_hbm(array):
    return pltpu.with_memory_space_constraint(array, pltpu.HBM)


def whole(array):
    return pl.BlockSpec(array.shape, lambda *ids: (0,) * array.ndim)


group_bytes = 2 * 32 * 32 * 256 * 4


def call_z_forward(phi, table):
    return pl.pallas_call(
        z_forward,
        grid=(2, groups),
        in_specs=[
            pl.BlockSpec((2, 32, 16, 128), lambda j, g: (g, 0, j, 0)),
            pl.BlockSpec((2, 32, 16, 128), lambda j, g: (g, 0, j, 1)),
            whole(table),
        ],
        out_specs=[
            pl.BlockSpec((128, 2, 8, 128), lambda j, g: (0, g, j, 0)),
            pl.BlockSpec((32, 16, 256), lambda j, g: (0, j, 0)),
        ],
        out_shape=[hbm((128, 2 * groups, 16, 128)), hbm((32, 32, 256))],
        compiler_params=params(2),
        cost_estimate=cost(2.4e9, 2 * groups * group_bytes),
        name="z_forward",
    )(phi, phi, table)


smem = pl.BlockSpec(memory_space=pltpu.SMEM)
anywhere = pl.BlockSpec(memory_space=pl.ANY)


def call_middle(coefs, spec, tables):
    shapes = [
        pltpu.VMEM((2, 64, 2, 16, 128), jnp.float32),
        *[pltpu.VMEM(table.shape, jnp.bfloat16) for table in tables],
        pltpu.VMEM((4 * groups, 256, 512), jnp.float32),
        pltpu.VMEM((2, 512, 768), jnp.bfloat16),
        pltpu.VMEM((2, 64, 2, 16, 128), jnp.float32),
        pltpu.SemaphoreType.DMA((8,)),
    ]
    return pl.pallas_call(
        middle,
        in_specs=[smem] + [anywhere] * (1 + len(tables)),
        out_specs=anywhere,
        out_shape=hbm(spec.shape),
        scratch_shapes=shapes,
        compiler_params=pltpu.CompilerParams(vmem_limit_bytes=vmem_bytes),
        cost_estimate=cost(20e9, 6 * groups * group_bytes),
        name="middle",
    )(coefs, spec, *tables)


def call_z_back(spec, phi, own, partner, table):
    return pl.pallas_call(
        z_back,
        grid=(2, groups),
        in_specs=[
            pl.BlockSpec((128, 2, 8, 128), lambda j, g: (0, g, j, 0)),
            pl.BlockSpec((2, 32, 16, 256), lambda j, g: (g, 0, j, 0)),
            pl.BlockSpec((32, 16, 256), lambda j, g: (0, j, 0)),
            pl.BlockSpec((32, 16, 256), lambda j, g: (0, j, 0)),
            whole(table),
        ],
        out_specs=pl.BlockSpec((2, 32, 16, 256), lambda j, g: (g, 0, j, 0)),
        out_shape=hbm(phi.shape),
        scratch_shapes=[pltpu.VMEM((2, 2, 32, 16, 128), jnp.float32)],
        compiler_params=params(2),
        cost_estimate=cost(2.4e9, 3 * groups * group_bytes),
        name="z_back",
    )(spec, phi, in_hbm(own), in_hbm(partner), table)


def exchange(block):
    return lax.all_to_all(block, every, split_axis=0, concat_axis=0, tiled=True)


def coefficients(strains, variant_strain, variants):
    bank_rows = strains.shape[0]
    picked = variant_strain[:variants]
    one_hot = (picked[:, None] == jnp.arange(bank_rows, dtype=jnp.int32)[None, :]).astype(
        jnp.float32
    )
    chosen = jnp.dot(one_hot, strains, precision=highest)
    trace = lame_first * (chosen[:, 0] + chosen[:, 1] + chosen[:, 2])
    diagonal = jnp.asarray([1.0, 1.0, 1.0, 0.0, 0.0, 0.0], jnp.float32)
    stress = trace[:, None] * diagonal[None, :] + 2.0 * shear_mod * chosen
    plane = lax.axis_index(every).astype(jnp.float32)
    last = jnp.full((1, 12), plane, jnp.float32)
    return jnp.concatenate([jnp.concatenate([chosen, stress], axis=1), last], axis=0)


def shards(order_field, strains, variant_strain):
    length = order_field.shape[3]
    tables = [in_hbm(jnp.asarray(table)) for table in dft_tables(length)]
    z_fwd, z_inv, y_fwd, y_inv, x_fwd, x_inv = tables
    coefs = coefficients(strains, variant_strain, 12)
    sent, squares = call_z_forward(order_field, z_fwd)
    arrived = exchange(sent)
    squares, arrived = lax.optimization_barrier((squares, arrived))
    partner = lax.ppermute(squares, "var", [(0, 1), (1, 0)])
    sent = call_middle(coefs, arrived, (y_fwd, x_fwd, x_inv, y_inv))
    sent, partner = lax.optimization_barrier((sent, partner))
    returned = exchange(sent)
    return call_z_back(returned, order_field, squares, partner, z_inv)


def solution(mesh):
    placed = (P("var", "py", "pz", None), P(), P())
    return jax.shard_map(
        shards, mesh=mesh, in_specs=placed, out_specs=P("var", "py", "pz", None), check_vma=False
    )
```

```python
import functools

import jax
import jax.numpy as jnp
import ml_dtypes
import numpy as np
from jax import lax
from jax.experimental import pallas as pl
from jax.experimental.pallas import tpu as pltpu
from jax.sharding import PartitionSpec as P

lame_first = 1.5
shear_mod = 1.0
relax_coef = 1.0 / 1.4
grad_coef = 0.5
mobility = 0.2
landau_cubic = 3.0
landau_quartic = 0.5
two_pi = 6.283185307179586
highest = lax.Precision.HIGHEST
every = ("var", "pz", "py")
vmem_bytes = 48 * 1024 * 1024

groups = 3


def split_table(table):
    high = table.astype(ml_dtypes.bfloat16)
    low = (table - high.astype(np.float64)).astype(ml_dtypes.bfloat16)
    return high, low


def left_table(table):
    return np.concatenate(split_table(table), axis=1)


def right_table(table):
    return np.concatenate(split_table(table), axis=0)


def complex_blocks(angles, sign):
    cos, sin = np.cos(angles), sign * np.sin(angles)
    table = np.empty((2, angles.shape[0], 2, angles.shape[1]))
    table[0, :, 0], table[0, :, 1] = cos, sin
    table[1, :, 0], table[1, :, 1] = -sin, cos
    return table


@functools.cache
def dft_tables(length):
    half = length // 2
    ids = np.arange(length)
    unit = 2.0 * np.pi / length
    angles = (ids[:, None] * ids[None, :] % length) * unit
    cos, sin = np.cos(angles), np.sin(angles)
    z_fwd = left_table(np.concatenate([cos[:half], -sin[:half]], axis=0))
    weight = -mobility * np.where(np.arange(half) == 0, 1.0, 2.0)[:, None]
    z_back = right_table(np.concatenate([cos[:half] * weight, -sin[:half] * weight], axis=0))
    low = np.arange(half)
    blocks = 8
    width = length // blocks
    y_fwd, y_back, x_fwd, x_back = [], [], [], []
    for parity in range(2):
        y_ids = 2 * low + parity
        fwd = complex_blocks((y_ids[:, None] * low[None, :] % length) * unit, -1.0)
        fwd = fwd.reshape(2, blocks, width // 2, length)
        y_fwd.append(left_table(fwd.transpose(3, 1, 0, 2).reshape(length, length)))
        back = complex_blocks((low[:, None] * y_ids[None, :] % length) * unit, 1.0)
        back = back.reshape(length, 2, blocks, width // 2)
        y_back.append(left_table(back.transpose(2, 1, 3, 0).reshape(length, length)))
        x_ids = low.reshape(2, 2, width).transpose(1, 0, 2).reshape(half)
        k_ids = 2 * low + parity
        fwd = complex_blocks((x_ids[:, None] * k_ids[None, :] % length) * unit, -1.0)
        x_fwd.append(right_table(fwd.reshape(length, length)))
        back = complex_blocks((k_ids[:, None] * x_ids[None, :] % length) * unit, 1.0)
        x_back.append(right_table(back.reshape(length, length)))
    return z_fwd, z_back, np.stack(y_fwd), np.stack(y_back), np.stack(x_fwd), np.stack(x_back)


def split_value(value):
    high = value.astype(jnp.bfloat16)
    low = (value - high.astype(jnp.float32)).astype(jnp.bfloat16)
    return high, low


def as_left(value):
    high, low = split_value(value)
    return jnp.concatenate([high, low, high], axis=1)


def as_right_tr(value):
    high, low = split_value(value)
    return jnp.concatenate([high, high, low], axis=1)


def as_right(value):
    high, low = split_value(value)
    return jnp.concatenate([high, high, low], axis=0)


def left_rows(table):
    width = table.shape[1] // 2
    return jnp.concatenate([table, table[:, :width]], axis=1)


def right_rows(table):
    depth = table.shape[0] // 2
    return jnp.concatenate([table[:depth], table], axis=0)


def matmul(left, right):
    return lax.dot_general(
        left, right, (((1,), (0,)), ((), ())), preferred_element_type=jnp.float32
    )


def matmul_tr(left, right):
    return lax.dot_general(
        left, right, (((1,), (1,)), ((), ())), preferred_element_type=jnp.float32
    )


def lane_ids(rows):
    return lax.broadcasted_iota(jnp.int32, (rows, 128), 1)


def z_pieces(spec_hbm, spec_ref, grid_hbm, grid_ref, sems):
    def spec(step, back):
        group, part = step // 2 * 2, pl.multiple_of(step % 2 * 8, 8)
        place = (slice(None), pl.ds(group, 2), pl.ds(part, 8))
        ends = [spec_hbm.at[place], spec_ref.at[step, :, pl.ds(0, 2)]]
        return pltpu.make_async_copy(*(ends[::-1] if back else ends), sems.at[0, step])

    def grid(step, side, back):
        group, part = step // 2 * 2, pl.multiple_of(step % 2 * 16, 16)
        place = (pl.ds(group, 2), slice(None), pl.ds(part, 16))
        ends = [
            grid_hbm.at[place + (pl.ds(side * 128, 128),)],
            grid_ref.at[step, side, :, :, pl.ds(0, 16)],
        ]
        number = (2 if back else 0) + 1 + side
        return pltpu.make_async_copy(*(ends[::-1] if back else ends), sems.at[number, step])

    return spec, grid


def z_forward(table_ref, phi_hbm, out_hbm, sq_hbm, phi_ref, out_ref, sq_ref, sems):
    spec, grid = z_pieces(out_hbm, out_ref, phi_hbm, phi_ref, sems)
    steps = groups * 2
    for step in range(steps):
        for side in range(2):
            grid(step, side, False).start()
    sq_ref[...] = jnp.zeros_like(sq_ref)
    rows_ref = phi_ref.reshape(steps * 3072, 128)
    flat_ref = out_ref.reshape(steps * 3072, 128)

    def body(step, carry):
        part_y = step % 2
        for side in range(2):
            grid(step, side, False).wait()
        base = pl.multiple_of(step * 3072, 8)
        for batch in range(4):
            block = jnp.concatenate(
                [
                    jnp.concatenate(
                        [
                            rows_ref[pl.ds(base + side * 1536 + batch * 4 + y, 64, stride=24), :]
                            for side in range(2)
                        ],
                        axis=1,
                    )
                    for y in range(4)
                ],
                axis=0,
            )
            spectrum = matmul_tr(left_rows(table_ref[...]), as_right_tr(block))
            for pair in range(2):
                for part in range(2):
                    start = base + part * 8 + batch * 2 + pair
                    flat_ref[pl.ds(start, 128, stride=24), :] = spectrum[
                        part * 128 : part * 128 + 128, pair * 128 : pair * 128 + 128
                    ]
        spec(step, True).start()
        ys = pl.ds(pl.multiple_of(part_y * 16, 16), 16)
        for side in range(2):
            lanes = slice(side * 128, side * 128 + 128)
            one, two = [phi_ref[step, side, v, :, 0:16, :] for v in range(2)]
            sq_ref[:, ys, lanes] += one * one + two * two
        return carry

    lax.fori_loop(0, steps, body, 0)
    last = pltpu.make_async_copy(sq_ref, sq_hbm, sems.at[3, 0])
    last.start()
    for step in range(steps):
        spec(step, True).wait()
    last.wait()


def transform_there(in_ref, y_ref, x_ref, out_ref, left_ref):
    lanes = lane_ids(256)
    low_half = lanes < 64
    first_bit = lane_ids(128) // 32 % 2 == 0
    halves = []
    for pp in range(2):
        evens, odds = [], []
        for place in (pp, pp + 2):
            first, second = [
                jnp.concatenate(
                    [in_ref[pz * 8 + place * 2 + side].reshape(32, 128) for pz in range(8)], axis=0
                )
                for side in range(2)
            ]
            evens.append(jnp.where(low_half, first, pltpu.roll(second, 64, 1)))
            odds.append(jnp.where(low_half, pltpu.roll(first, 64, 1), second))
        even = matmul(left_rows(y_ref[0]), as_right(jnp.concatenate(evens, axis=1)))
        odd = matmul(left_rows(y_ref[1]), as_right(jnp.concatenate(odds, axis=1)))
        low, high = even + odd, even - odd
        halves.append(
            [
                [side[:, :128] + side[:, 128:], side[:, :128] - side[:, 128:]]
                for side in (low, high)
            ]
        )
    for parity in range(2):
        for side in range(2):
            for part in range(2):
                rows = slice(part * 128, part * 128 + 128)
                zero = halves[0][side][parity][rows]
                one = halves[1][side][parity][rows]
                values = (
                    jnp.where(first_bit, zero, pltpu.roll(one, 32, 1)),
                    jnp.where(first_bit, pltpu.roll(zero, 96, 1), one),
                )
                for v, value in enumerate(values):
                    high, low = split_value(value)
                    start = v * 256 + side * 128
                    for third, piece in enumerate((high, low, high)):
                        column = third * 256 + part * 128
                        left_ref[parity, start : start + 128, column : column + 128] = piece
    for parity in range(2):
        product = matmul(left_ref[parity], right_rows(x_ref[parity]))
        for v in range(2):
            out_ref[v, :, parity * 256 : parity * 256 + 256] = product[v * 256 : v * 256 + 256]


def transform_back(in_ref, x_ref, y_ref, out_ref):
    lanes = lane_ids(256)
    low_half = lanes < 64
    first_bit = lanes // 32 % 2 == 0
    products = []
    for parity in range(2):
        columns = slice(parity * 256, parity * 256 + 256)
        block = jnp.concatenate([in_ref[0, :, columns], in_ref[1, :, columns]], axis=0)
        products.append(matmul(as_left(block), right_rows(x_ref[parity])))
    for side in range(2):
        field = products[0] + products[1] if side == 0 else products[0] - products[1]
        evens, odds = ([], []), ([], [])
        for part in range(2):
            zero = field[:256, part * 128 : part * 128 + 128]
            one = field[256:, part * 128 : part * 128 + 128]
            merged = (
                jnp.where(first_bit, zero, pltpu.roll(one, 32, 1)),
                jnp.where(first_bit, pltpu.roll(zero, 96, 1), one),
            )
            for pp in range(2):
                evens[pp].append(merged[pp][:128] + merged[pp][128:])
                odds[pp].append(merged[pp][:128] - merged[pp][128:])
        results = []
        for parity, pieces in enumerate((evens, odds)):
            right = jnp.concatenate([jnp.concatenate(p, axis=0) for p in pieces], axis=1)
            results.append(matmul(left_rows(y_ref[parity]), as_right(right)))
        for pp in range(2):
            even = results[0][:, pp * 128 : pp * 128 + 128]
            odd = results[1][:, pp * 128 : pp * 128 + 128]
            place = (side * 2 + pp) * 2
            first = jnp.where(low_half, even, pltpu.roll(odd, 64, 1))
            second = jnp.where(low_half, pltpu.roll(even, 64, 1), odd)
            for pz in range(8):
                rows = slice(pz * 32, pz * 32 + 32)
                out_ref[pz * 8 + place] = first[rows].reshape(2, 16, 128)
                out_ref[pz * 8 + place + 1] = second[rows].reshape(2, 16, 128)


def waves(row, wave_z, length):
    half = length // 2
    ky = lax.broadcasted_iota(jnp.int32, (8, length), 0) + row
    column = lax.broadcasted_iota(jnp.int32, (8, length), 1)
    kx = column % half * 2 + column // half
    wy = jnp.where(ky >= half, ky - length, ky).astype(jnp.float32)
    wx = jnp.where(kx >= half, kx - length, kx).astype(jnp.float32)
    wz = jnp.full((8, length), wave_z, jnp.float32)
    squared = wx * wx + wy * wy + wz * wz
    volume = 1.0 / float(length * length * length)
    keep = jnp.where((ky == half) | (kx == half), 0.0, volume)
    grad = keep * squared * (grad_coef * (two_pi / length) ** 2)
    return wx, wy, wz, squared, keep, join(grad, grad)


def pick(value, part):
    half = value.shape[1] // 4
    return jnp.concatenate(
        [value[:, c * half : (c + 1) * half] for c in (part, part + 2)], axis=1
    )


def join(real, imag):
    half = real.shape[1] // 2
    pieces = [real[:, :half], imag[:, :half], real[:, half:], imag[:, half:]]
    return jnp.concatenate(pieces, axis=1)


def driving(strain, wx, wy, wz, squared, keep):
    inverse = 1.0 / jnp.maximum(squared, 1.0)
    trace = lame_first * (strain[0] + strain[1] + strain[2])
    s11 = trace + 2.0 * shear_mod * strain[0]
    s22 = trace + 2.0 * shear_mod * strain[1]
    s33 = trace + 2.0 * shear_mod * strain[2]
    s23 = 2.0 * shear_mod * strain[3]
    s13 = 2.0 * shear_mod * strain[4]
    s12 = 2.0 * shear_mod * strain[5]
    t1 = (s11 * wx + s12 * wy + s13 * wz) * inverse
    t2 = (s12 * wx + s22 * wy + s23 * wz) * inverse
    t3 = (s13 * wx + s23 * wy + s33 * wz) * inverse
    normal = (wx * t1 + wy * t2 + wz * t3) * (relax_coef * inverse)
    u1 = t1 - normal * wx
    u2 = t2 - normal * wy
    u3 = t3 - normal * wz
    return [
        keep * (strain[0] - wx * u1),
        keep * (strain[1] - wy * u2),
        keep * (strain[2] - wz * u3),
        keep * (2.0 * strain[3] - (wy * u3 + wz * u2)),
        keep * (2.0 * strain[4] - (wx * u3 + wz * u1)),
        keep * (2.0 * strain[5] - (wx * u2 + wy * u1)),
    ]


def middle(coef_ref, in_hbm, yf_hbm, xf_hbm, xb_hbm, yb_hbm, out_hbm, *scratch):
    in_ref, yf_ref, xf_ref, xb_ref, yb_ref, field_ref, left_ref, out_ref, sems = scratch
    length = field_ref.shape[1]
    wave_z = coef_ref[12, 0]
    steps = groups * 2

    def part_of(ref, step):
        return ref.at[
            pl.ds(pl.multiple_of(step % 2 * 64, 64), 64),
            pl.ds(pl.multiple_of(step // 2 * 2, 2), 2),
        ]

    def arrival(step):
        slot = step % 2
        return pltpu.make_async_copy(part_of(in_hbm, step), in_ref.at[slot], sems.at[slot])

    def departure(step):
        slot = step % 2
        return pltpu.make_async_copy(out_ref.at[slot], part_of(out_hbm, step), sems.at[2 + slot])

    moves = [(yf_hbm, yf_ref), (xf_hbm, xf_ref), (xb_hbm, xb_ref), (yb_hbm, yb_ref)]
    copies = [
        pltpu.make_async_copy(source, target, sems.at[4 + number])
        for number, (source, target) in enumerate(moves)
    ]
    copies[0].start()
    arrival(0).start()
    for copy in copies[1:]:
        copy.start()
    copies[0].wait()
    copies[1].wait()

    def there(step, carry):
        @pl.when(step + 1 < steps)
        def _():
            arrival(step + 1).start()

        arrival(step).wait()
        transform_there(
            in_ref.at[step % 2], yf_ref, xf_ref, field_ref.at[pl.ds(step * 2, 2)], left_ref
        )
        return carry

    lax.fori_loop(0, steps, there, 0)
    places = [(p % 6 // 2 * 2 + p // 6) * 2 + p % 2 for p in range(12)]

    def tile(step, carry):
        row = pl.multiple_of(step * 8, 8)
        rows = pl.ds(row, 8)
        wx, wy, wz, squared, keep, grad = waves(row, wave_z, length)
        strains = None
        for q, place in enumerate(places):
            value = field_ref[place, rows, :]
            terms = [coef_ref[q, m] * value for m in range(6)]
            strains = terms if q == 0 else [total + term for total, term in zip(strains, terms)]
        parts = [
            driving([pick(total, part) for total in strains], wx, wy, wz, squared, keep)
            for part in range(2)
        ]
        drive = [join(parts[0][m], parts[1][m]) for m in range(6)]
        for p, place in enumerate(places):
            total = grad * field_ref[place, rows, :]
            for m in range(6):
                total = total + coef_ref[p, 6 + m] * drive[m]
            field_ref[place, rows, :] = total
        return carry

    lax.fori_loop(0, length // 8, tile, 0)
    copies[2].wait()
    copies[3].wait()

    def back(step, carry):
        @pl.when(step >= 2)
        def _():
            departure(step - 2).wait()

        transform_back(field_ref.at[pl.ds(step * 2, 2)], xb_ref, yb_ref, out_ref.at[step % 2])
        departure(step).start()
        return carry

    lax.fori_loop(0, steps, back, 0)
    departure(steps - 2).wait()
    departure(steps - 1).wait()


def local_part(phi_ref, own_ref, partner_ref, out_ref):
    phi = phi_ref[...]
    total_sq = own_ref[...] + partner_ref[...]
    chemical = phi - landau_cubic * phi * phi + landau_quartic * phi * total_sq[None]
    out_ref[...] = phi - mobility * chemical


def z_back(table_ref, spec_hbm, base_hbm, out_hbm, spec_ref, base_ref, sems):
    spec, grid = z_pieces(spec_hbm, spec_ref, base_hbm, base_ref, sems)
    grid_out = z_pieces(spec_hbm, spec_ref, out_hbm, base_ref, sems)[1]
    steps = groups * 2
    for step in range(steps):
        spec(step, False).start()
        for side in range(2):
            grid(step, side, False).start()
    flat_ref = spec_ref.reshape(steps * 3072, 128)
    rows_ref = base_ref.reshape(steps * 3072, 128)

    def body(step, carry):
        base = pl.multiple_of(step * 3072, 8)
        spec(step, False).wait()
        for side in range(2):
            grid(step, side, False).wait()
        for batch in range(4):
            lefts = []
            for pair in range(2):
                turned = []
                for part in range(2):
                    start = base + part * 8 + batch * 2 + pair
                    turned.append(flat_ref[pl.ds(start, 128, stride=24), :].T)
                lefts.append(jnp.concatenate(turned, axis=1))
            force = matmul(as_left(jnp.concatenate(lefts, axis=0)), right_rows(table_ref[...]))
            for y in range(4):
                for side in range(2):
                    rows = pl.ds(base + side * 1536 + batch * 4 + y, 64, stride=24)
                    lanes = slice(side * 128, side * 128 + 128)
                    rows_ref[rows, :] = rows_ref[rows, :] + force[y * 64 : y * 64 + 64, lanes]
        for side in range(2):
            grid_out(step, side, True).start()
        return carry

    lax.fori_loop(0, steps, body, 0)
    for step in range(steps):
        for side in range(2):
            grid_out(step, side, True).wait()


def params(count):
    return pltpu.CompilerParams(
        dimension_semantics=("arbitrary",) * count, vmem_limit_bytes=vmem_bytes
    )


def cost(flops, moved):
    return pl.CostEstimate(flops=int(flops), bytes_accessed=int(moved), transcendentals=0)


def hbm(shape):
    return pltpu.HBM(shape, jnp.float32)


def in_hbm(array):
    return pltpu.with_memory_space_constraint(array, pltpu.HBM)


def whole(array):
    return pl.BlockSpec(array.shape, lambda *ids: (0,) * array.ndim)


group_bytes = 2 * 32 * 32 * 256 * 4


def call_z_forward(phi, table):
    return pl.pallas_call(
        z_forward,
        in_specs=[whole(table), anywhere],
        out_specs=[anywhere, anywhere],
        out_shape=[hbm((128, 2 * groups, 16, 128)), hbm((32, 32, 256))],
        scratch_shapes=[
            pltpu.VMEM((2 * groups, 2, 2, 32, 24, 128), jnp.float32),
            pltpu.VMEM((2 * groups, 128, 3, 8, 128), jnp.float32),
            pltpu.VMEM((32, 32, 256), jnp.float32),
            pltpu.SemaphoreType.DMA((5, 2 * groups)),
        ],
        compiler_params=pltpu.CompilerParams(vmem_limit_bytes=vmem_bytes),
        cost_estimate=cost(2.4e9, 2 * groups * group_bytes),
        name="z_forward",
    )(table, phi)


def call_local(phi, own, partner):
    return pl.pallas_call(
        local_part,
        grid=(groups, 4),
        in_specs=[
            pl.BlockSpec((2, 32, 8, 256), lambda g, j: (g, 0, j, 0)),
            pl.BlockSpec((32, 8, 256), lambda g, j: (0, j, 0)),
            pl.BlockSpec((32, 8, 256), lambda g, j: (0, j, 0)),
        ],
        out_specs=pl.BlockSpec((2, 32, 8, 256), lambda g, j: (g, 0, j, 0)),
        out_shape=hbm(phi.shape),
        compiler_params=params(2),
        cost_estimate=cost(50e6, 3 * groups * group_bytes),
        name="local_part",
    )(phi, in_hbm(own), in_hbm(partner))


smem = pl.BlockSpec(memory_space=pltpu.SMEM)
anywhere = pl.BlockSpec(memory_space=pl.ANY)


def call_middle(coefs, spec, tables):
    shapes = [
        pltpu.VMEM((2, 64, 2, 16, 128), jnp.float32),
        *[pltpu.VMEM(table.shape, jnp.bfloat16) for table in tables],
        pltpu.VMEM((4 * groups, 256, 512), jnp.float32),
        pltpu.VMEM((2, 512, 768), jnp.bfloat16),
        pltpu.VMEM((2, 64, 2, 16, 128), jnp.float32),
        pltpu.SemaphoreType.DMA((8,)),
    ]
    return pl.pallas_call(
        middle,
        in_specs=[smem] + [anywhere] * (1 + len(tables)),
        out_specs=anywhere,
        out_shape=hbm(spec.shape),
        scratch_shapes=shapes,
        compiler_params=pltpu.CompilerParams(vmem_limit_bytes=vmem_bytes),
        cost_estimate=cost(20e9, 6 * groups * group_bytes),
        name="middle",
    )(coefs, spec, *tables)


def call_z_back(spec, base, table):
    return pl.pallas_call(
        z_back,
        in_specs=[whole(table), anywhere, anywhere],
        out_specs=anywhere,
        out_shape=hbm(base.shape),
        scratch_shapes=[
            pltpu.VMEM((2 * groups, 128, 3, 8, 128), jnp.float32),
            pltpu.VMEM((2 * groups, 2, 2, 32, 24, 128), jnp.float32),
            pltpu.SemaphoreType.DMA((5, 2 * groups)),
        ],
        compiler_params=pltpu.CompilerParams(vmem_limit_bytes=vmem_bytes),
        cost_estimate=cost(2.4e9, 3 * groups * group_bytes),
        name="z_back",
    )(table, spec, in_hbm(base))


def exchange(block):
    return lax.all_to_all(block, every, split_axis=0, concat_axis=0, tiled=True)


def coefficients(strains, variant_strain, variants):
    bank_rows = strains.shape[0]
    picked = variant_strain[:variants]
    one_hot = (picked[:, None] == jnp.arange(bank_rows, dtype=jnp.int32)[None, :]).astype(
        jnp.float32
    )
    chosen = jnp.dot(one_hot, strains, precision=highest)
    trace = lame_first * (chosen[:, 0] + chosen[:, 1] + chosen[:, 2])
    diagonal = jnp.asarray([1.0, 1.0, 1.0, 0.0, 0.0, 0.0], jnp.float32)
    stress = trace[:, None] * diagonal[None, :] + 2.0 * shear_mod * chosen
    plane = lax.axis_index(every).astype(jnp.float32)
    last = jnp.full((1, 12), plane, jnp.float32)
    return jnp.concatenate([jnp.concatenate([chosen, stress], axis=1), last], axis=0)


def shards(order_field, strains, variant_strain):
    length = order_field.shape[3]
    tables = [in_hbm(jnp.asarray(table)) for table in dft_tables(length)]
    z_fwd, z_inv, y_fwd, y_inv, x_fwd, x_inv = tables
    coefs = coefficients(strains, variant_strain, 12)
    sent, squares = call_z_forward(order_field, z_fwd)
    arrived = exchange(sent)
    squares, arrived = lax.optimization_barrier((squares, arrived))
    partner = lax.ppermute(squares, "var", [(0, 1), (1, 0)])
    sent = call_middle(coefs, arrived, (y_fwd, x_fwd, x_inv, y_inv))
    sent, partner = lax.optimization_barrier((sent, partner))
    returned = exchange(sent)
    base = call_local(order_field, squares, partner)
    return call_z_back(returned, base, z_inv)


def solution(mesh):
    placed = (P("var", "py", "pz", None), P(), P())
    return jax.shard_map(
        shards, mesh=mesh, in_specs=placed, out_specs=P("var", "py", "pz", None), check_vma=False
    )
```

```python
import functools

import jax
import jax.numpy as jnp
import ml_dtypes
import numpy as np
from jax import lax
from jax.experimental import pallas as pl
from jax.experimental.pallas import tpu as pltpu
from jax.sharding import PartitionSpec as P

lame_first = 1.5
shear_mod = 1.0
relax_coef = 1.0 / 1.4
grad_coef = 0.5
mobility = 0.2
landau_cubic = 3.0
landau_quartic = 0.5
two_pi = 6.283185307179586
highest = lax.Precision.HIGHEST
every = ("var", "pz", "py")
vmem_bytes = 36 * 1024 * 1024

groups = 3


def split_table(table):
    high = table.astype(ml_dtypes.bfloat16)
    low = (table - high.astype(np.float64)).astype(ml_dtypes.bfloat16)
    return high, low


def left_table(table):
    return np.concatenate(split_table(table), axis=1)


def right_table(table):
    return np.concatenate(split_table(table), axis=0)


def complex_blocks(angles, sign):
    cos, sin = np.cos(angles), sign * np.sin(angles)
    table = np.empty((2, angles.shape[0], 2, angles.shape[1]))
    table[0, :, 0], table[0, :, 1] = cos, sin
    table[1, :, 0], table[1, :, 1] = -sin, cos
    return table


@functools.cache
def dft_tables(length):
    half = length // 2
    ids = np.arange(length)
    unit = 2.0 * np.pi / length
    angles = (ids[:, None] * ids[None, :] % length) * unit
    cos, sin = np.cos(angles), np.sin(angles)
    z_fwd = left_table(np.concatenate([cos[:half], -sin[:half]], axis=0))
    weight = -mobility * np.where(np.arange(half) == 0, 1.0, 2.0)[:, None]
    z_back = right_table(np.concatenate([cos[:half] * weight, -sin[:half] * weight], axis=0))
    low = np.arange(half)
    blocks = 8
    width = length // blocks
    y_fwd, y_back, x_fwd, x_back = [], [], [], []
    for parity in range(2):
        y_ids = 2 * low + parity
        fwd = complex_blocks((y_ids[:, None] * low[None, :] % length) * unit, -1.0)
        fwd = fwd.reshape(2, blocks, width // 2, length)
        y_fwd.append(left_table(fwd.transpose(3, 1, 0, 2).reshape(length, length)))
        back = complex_blocks((low[:, None] * y_ids[None, :] % length) * unit, 1.0)
        back = back.reshape(length, 2, blocks, width // 2)
        y_back.append(left_table(back.transpose(2, 1, 3, 0).reshape(length, length)))
        x_ids = low.reshape(2, 2, width).transpose(1, 0, 2).reshape(half)
        k_ids = 2 * low + parity
        fwd = complex_blocks((x_ids[:, None] * k_ids[None, :] % length) * unit, -1.0)
        x_fwd.append(right_table(fwd.reshape(length, length)))
        back = complex_blocks((k_ids[:, None] * x_ids[None, :] % length) * unit, 1.0)
        x_back.append(right_table(back.reshape(length, length)))
    return z_fwd, z_back, np.stack(y_fwd), np.stack(y_back), np.stack(x_fwd), np.stack(x_back)


def split_value(value):
    high = value.astype(jnp.bfloat16)
    low = (value - high.astype(jnp.float32)).astype(jnp.bfloat16)
    return high, low


def as_left(value):
    high, low = split_value(value)
    return jnp.concatenate([high, low, high], axis=1)


def as_right_tr(value):
    high, low = split_value(value)
    return jnp.concatenate([high, high, low], axis=1)


def as_right(value):
    high, low = split_value(value)
    return jnp.concatenate([high, high, low], axis=0)


def left_rows(table):
    width = table.shape[1] // 2
    return jnp.concatenate([table, table[:, :width]], axis=1)


def right_rows(table):
    depth = table.shape[0] // 2
    return jnp.concatenate([table[:depth], table], axis=0)


def matmul(left, right):
    return lax.dot_general(
        left, right, (((1,), (0,)), ((), ())), preferred_element_type=jnp.float32
    )


def matmul_tr(left, right):
    return lax.dot_general(
        left, right, (((1,), (1,)), ((), ())), preferred_element_type=jnp.float32
    )


def lane_ids(rows):
    return lax.broadcasted_iota(jnp.int32, (rows, 128), 1)


def z_pieces(spec_hbm, spec_ref, grid_hbm, grid_ref, sems):
    def spec(step, back):
        group, part = step // 2 * 2, pl.multiple_of(step % 2 * 8, 8)
        place = (slice(None), pl.ds(group, 2), pl.ds(part, 8))
        ends = [spec_hbm.at[place], spec_ref.at[step, :, pl.ds(0, 2)]]
        return pltpu.make_async_copy(*(ends[::-1] if back else ends), sems.at[0, step])

    def grid(step, side, back):
        group, part = step // 2 * 2, pl.multiple_of(step % 2 * 16, 16)
        place = (pl.ds(group, 2), slice(None), pl.ds(part, 16))
        ends = [
            grid_hbm.at[place + (pl.ds(side * 128, 128),)],
            grid_ref.at[step, side, :, :, pl.ds(0, 16)],
        ]
        number = (2 if back else 0) + 1 + side
        return pltpu.make_async_copy(*(ends[::-1] if back else ends), sems.at[number, step])

    return spec, grid


def z_forward(table_hbm, phi_hbm, out_hbm, sq_hbm, table_ref, phi_ref, out_ref, sq_ref, sems):
    spec, grid = z_pieces(out_hbm, out_ref, phi_hbm, phi_ref, sems)
    steps = groups * 2
    table = pltpu.make_async_copy(table_hbm, table_ref, sems.at[4, 0])
    table.start()
    for step in range(steps):
        for side in range(2):
            grid(step, side, False).start()
    table.wait()
    sq_ref[...] = jnp.zeros_like(sq_ref)
    rows_ref = phi_ref.reshape(steps * 3072, 128)
    flat_ref = out_ref.reshape(steps * 3072, 128)

    def body(step, carry):
        part_y = step % 2
        for side in range(2):
            grid(step, side, False).wait()
        base = pl.multiple_of(step * 3072, 8)
        for batch in range(4):
            block = jnp.concatenate(
                [
                    jnp.concatenate(
                        [
                            rows_ref[pl.ds(base + side * 1536 + batch * 4 + y, 64, stride=24), :]
                            for side in range(2)
                        ],
                        axis=1,
                    )
                    for y in range(4)
                ],
                axis=0,
            )
            spectrum = matmul_tr(left_rows(table_ref[...]), as_right_tr(block))
            for pair in range(2):
                for part in range(2):
                    start = base + part * 8 + batch * 2 + pair
                    flat_ref[pl.ds(start, 128, stride=24), :] = spectrum[
                        part * 128 : part * 128 + 128, pair * 128 : pair * 128 + 128
                    ]
        spec(step, True).start()
        ys = pl.ds(pl.multiple_of(part_y * 16, 16), 16)
        for side in range(2):
            lanes = slice(side * 128, side * 128 + 128)
            one, two = [phi_ref[step, side, v, :, 0:16, :] for v in range(2)]
            sq_ref[:, ys, lanes] += one * one + two * two
        return carry

    lax.fori_loop(0, steps, body, 0)
    last = pltpu.make_async_copy(sq_ref, sq_hbm, sems.at[3, 0])
    last.start()
    for step in range(steps):
        spec(step, True).wait()
    last.wait()


def y_there(in_ref, y_ref, left_ref):
    lanes = lane_ids(256)
    low_half = lanes < 64
    first_bit = lane_ids(128) // 32 % 2 == 0
    halves = []
    for pp in range(2):
        evens, odds = [], []
        for place in (pp, pp + 2):
            first, second = [
                jnp.concatenate(
                    [in_ref[pz * 8 + place * 2 + side].reshape(32, 128) for pz in range(8)], axis=0
                )
                for side in range(2)
            ]
            evens.append(jnp.where(low_half, first, pltpu.roll(second, 64, 1)))
            odds.append(jnp.where(low_half, pltpu.roll(first, 64, 1), second))
        even = matmul(left_rows(y_ref[0]), as_right(jnp.concatenate(evens, axis=1)))
        odd = matmul(left_rows(y_ref[1]), as_right(jnp.concatenate(odds, axis=1)))
        low, high = even + odd, even - odd
        halves.append(
            [
                [side[:, :128] + side[:, 128:], side[:, :128] - side[:, 128:]]
                for side in (low, high)
            ]
        )
    for parity in range(2):
        for side in range(2):
            for part in range(2):
                rows = slice(part * 128, part * 128 + 128)
                zero = halves[0][side][parity][rows]
                one = halves[1][side][parity][rows]
                values = (
                    jnp.where(first_bit, zero, pltpu.roll(one, 32, 1)),
                    jnp.where(first_bit, pltpu.roll(zero, 96, 1), one),
                )
                for v, value in enumerate(values):
                    high, low = split_value(value)
                    start = v * 256 + side * 128
                    for place, piece in enumerate((high, low)):
                        column = place * 256 + part * 128
                        left_ref[parity, start : start + 128, column : column + 128] = piece


def x_there(left_ref, x_ref, out_ref):
    for parity in range(2):
        product = matmul(left_rows(left_ref[parity]), right_rows(x_ref[parity]))
        for v in range(2):
            out_ref[v, :, parity * 256 : parity * 256 + 256] = product[v * 256 : v * 256 + 256]


def x_back(in_ref, x_ref, mid_ref):
    products = []
    for parity in range(2):
        columns = slice(parity * 256, parity * 256 + 256)
        block = jnp.concatenate([in_ref[0, :, columns], in_ref[1, :, columns]], axis=0)
        products.append(matmul(as_left(block), right_rows(x_ref[parity])))
    mid_ref[0] = products[0] + products[1]
    mid_ref[1] = products[0] - products[1]


def y_back(mid_ref, y_ref, out_ref):
    lanes = lane_ids(256)
    low_half = lanes < 64
    first_bit = lanes // 32 % 2 == 0
    for side in range(2):
        evens, odds = ([], []), ([], [])
        for part in range(2):
            zero = mid_ref[side, :256, part * 128 : part * 128 + 128]
            one = mid_ref[side, 256:, part * 128 : part * 128 + 128]
            merged = (
                jnp.where(first_bit, zero, pltpu.roll(one, 32, 1)),
                jnp.where(first_bit, pltpu.roll(zero, 96, 1), one),
            )
            for pp in range(2):
                evens[pp].append(merged[pp][:128] + merged[pp][128:])
                odds[pp].append(merged[pp][:128] - merged[pp][128:])
        results = []
        for parity, pieces in enumerate((evens, odds)):
            right = jnp.concatenate([jnp.concatenate(p, axis=0) for p in pieces], axis=1)
            results.append(matmul(left_rows(y_ref[parity]), as_right(right)))
        for pp in range(2):
            even = results[0][:, pp * 128 : pp * 128 + 128]
            odd = results[1][:, pp * 128 : pp * 128 + 128]
            place = (side * 2 + pp) * 2
            first = jnp.where(low_half, even, pltpu.roll(odd, 64, 1))
            second = jnp.where(low_half, pltpu.roll(even, 64, 1), odd)
            for pz in range(8):
                rows = slice(pz * 32, pz * 32 + 32)
                out_ref[pz * 8 + place] = first[rows].reshape(2, 16, 128)
                out_ref[pz * 8 + place + 1] = second[rows].reshape(2, 16, 128)


def signed_index(indices, length):
    half = length // 2
    return jnp.where(indices >= half, indices - length, indices).astype(jnp.float32)


def waves_x(wave_z, length):
    half = length // 2
    column = lax.broadcasted_iota(jnp.int32, (8, length), 1)
    kx = jnp.where(column >= half, column * 2 - (length - 1), column * 2)
    wx = signed_index(kx, length)
    keep = jnp.where(kx == half, 0.0, 1.0 / float(length * length * length))
    return wx, wx * wx + wave_z * wave_z, keep


def waves_y(row, length):
    ky = lax.broadcasted_iota(jnp.int32, (8, length), 0) + row
    return signed_index(ky, length), jnp.where(ky == length // 2, 0.0, 1.0)


def pick(value, part):
    half = value.shape[1] // 4
    return jnp.concatenate(
        [value[:, c * half : (c + 1) * half] for c in (part, part + 2)], axis=1
    )


def join(real, imag):
    half = real.shape[1] // 2
    pieces = [real[:, :half], imag[:, :half], real[:, half:], imag[:, half:]]
    return jnp.concatenate(pieces, axis=1)


def driving(strain, wx, wy, wz, squared, keep):
    inverse = 1.0 / jnp.maximum(squared, 1.0)
    trace = lame_first * (strain[0] + strain[1] + strain[2])
    s11 = trace + 2.0 * shear_mod * strain[0]
    s22 = trace + 2.0 * shear_mod * strain[1]
    s33 = trace + 2.0 * shear_mod * strain[2]
    s23 = 2.0 * shear_mod * strain[3]
    s13 = 2.0 * shear_mod * strain[4]
    s12 = 2.0 * shear_mod * strain[5]
    t1 = (s11 * wx + s12 * wy + s13 * wz) * inverse
    t2 = (s12 * wx + s22 * wy + s23 * wz) * inverse
    t3 = (s13 * wx + s23 * wy + s33 * wz) * inverse
    normal = (wx * t1 + wy * t2 + wz * t3) * (relax_coef * inverse)
    u1 = t1 - normal * wx
    u2 = t2 - normal * wy
    u3 = t3 - normal * wz
    return [
        keep * (strain[0] - wx * u1),
        keep * (strain[1] - wy * u2),
        keep * (strain[2] - wz * u3),
        keep * (2.0 * strain[3] - (wy * u3 + wz * u2)),
        keep * (2.0 * strain[4] - (wx * u3 + wz * u1)),
        keep * (2.0 * strain[5] - (wx * u2 + wy * u1)),
    ]


def middle(coef_hbm, in_ref, yf_hbm, xf_hbm, xb_hbm, yb_hbm, out_hbm, *scratch):
    yf_ref, xf_ref, xb_ref, yb_ref, coef_ref, field_ref, lefts, mids, out_ref, sems = scratch
    length = field_ref.shape[1]
    steps = groups * 2

    def part_of(ref, step):
        return ref.at[
            pl.ds(pl.multiple_of(step % 2 * 64, 64), 64),
            pl.ds(pl.multiple_of(step // 2 * 2, 2), 2),
        ]

    def departure(step):
        return pltpu.make_async_copy(out_ref.at[step], part_of(out_hbm, step), sems.at[1, step])

    def fields_of(step):
        return field_ref.at[pl.ds(step * 2, 2)]

    moves = [(yf_hbm, yf_ref), (xf_hbm, xf_ref), (xb_hbm, xb_ref), (yb_hbm, yb_ref)]
    moves.append((coef_hbm, coef_ref))
    copies = [
        pltpu.make_async_copy(source, target, sems.at[0, number])
        for number, (source, target) in enumerate(moves)
    ]
    for copy in copies:
        copy.start()

    def there_first(step, slot):
        y_there(part_of(in_ref, step), yf_ref, lefts[slot])

    def there_second(step, slot):
        x_there(lefts[slot], xf_ref, fields_of(step))

    copies[0].wait()
    there_first(0, 0)
    copies[1].wait()

    def there(turn, carry):
        for slot in range(2):
            there_first(turn * 2 + slot + 1, 1 - slot)
            there_second(turn * 2 + slot, slot)
        return carry

    lax.fori_loop(0, groups - 1, there, 0)
    there_first(steps - 1, 1)
    there_second(steps - 2, 0)
    there_second(steps - 1, 1)
    copies[4].wait()
    wave_z = coef_ref[12, 0]
    places = [(p % 6 // 2 * 2 + p // 6) * 2 + p % 2 for p in range(12)]

    wx, squared_xz, keep_x = waves_x(wave_z, length)

    def tile(step, carry):
        row = pl.multiple_of(step * 8, 8)
        rows = pl.ds(row, 8)
        wy, keep_y = waves_y(row, length)
        squared = squared_xz + wy * wy
        keep = keep_x * keep_y
        half_grad = keep * squared * (grad_coef * (two_pi / length) ** 2)
        grad = join(half_grad, half_grad)
        strains = None
        for q, place in enumerate(places):
            value = field_ref[place, rows, :]
            terms = [coef_ref[q, m] * value for m in range(6)]
            strains = terms if q == 0 else [total + term for total, term in zip(strains, terms)]
        parts = [
            driving([pick(total, part) for total in strains], wx, wy, wave_z, squared, keep)
            for part in range(2)
        ]
        drive = [join(parts[0][m], parts[1][m]) for m in range(6)]
        for p, place in enumerate(places):
            total = grad * field_ref[place, rows, :]
            for m in range(6):
                total = total + coef_ref[p, 6 + m] * drive[m]
            field_ref[place, rows, :] = total
        return carry

    lax.fori_loop(0, length // 8, tile, 0)
    copies[2].wait()
    copies[3].wait()

    def back_first(step, slot):
        x_back(fields_of(step), xb_ref, mids[slot])

    def back_second(step, slot):
        y_back(mids[slot], yb_ref, out_ref.at[step])
        departure(step).start()

    back_first(0, 0)

    def back(turn, carry):
        for slot in range(2):
            back_first(turn * 2 + slot + 1, 1 - slot)
            back_second(turn * 2 + slot, slot)
        return carry

    lax.fori_loop(0, groups - 1, back, 0)
    back_first(steps - 1, 1)
    back_second(steps - 2, 0)
    back_second(steps - 1, 1)
    for step in range(steps):
        departure(step).wait()


def local_part(phi_ref, own_ref, partner_ref, out_ref):
    phi = phi_ref[...]
    total_sq = own_ref[...] + partner_ref[...]
    chemical = phi - landau_cubic * phi * phi + landau_quartic * phi * total_sq[None]
    out_ref[...] = phi - mobility * chemical


def z_back(table_hbm, spec_hbm, base_hbm, out_hbm, table_ref, spec_ref, base_ref, sems):
    spec, grid = z_pieces(spec_hbm, spec_ref, base_hbm, base_ref, sems)
    grid_out = z_pieces(spec_hbm, spec_ref, out_hbm, base_ref, sems)[1]
    steps = groups * 2
    table = pltpu.make_async_copy(table_hbm, table_ref, sems.at[5, 0])
    for step in range(steps):
        spec(step, False).start()
        for side in range(2):
            grid(step, side, False).start()
        if step == 0:
            table.start()
    table.wait()
    flat_ref = spec_ref.reshape(steps * 3072, 128)
    rows_ref = base_ref.reshape(steps * 3072, 128)

    def body(step, carry):
        base = pl.multiple_of(step * 3072, 8)
        spec(step, False).wait()
        for side in range(2):
            grid(step, side, False).wait()
        for batch in range(4):
            lefts = []
            for pair in range(2):
                turned = []
                for part in range(2):
                    start = base + part * 8 + batch * 2 + pair
                    turned.append(flat_ref[pl.ds(start, 128, stride=24), :].T)
                lefts.append(jnp.concatenate(turned, axis=1))
            force = matmul(as_left(jnp.concatenate(lefts, axis=0)), right_rows(table_ref[...]))
            for y in range(4):
                for side in range(2):
                    rows = pl.ds(base + side * 1536 + batch * 4 + y, 64, stride=24)
                    lanes = slice(side * 128, side * 128 + 128)
                    rows_ref[rows, :] = rows_ref[rows, :] + force[y * 64 : y * 64 + 64, lanes]
        for side in range(2):
            grid_out(step, side, True).start()
        return carry

    lax.fori_loop(0, steps, body, 0)
    for step in range(steps):
        for side in range(2):
            grid_out(step, side, True).wait()


def params(count):
    return pltpu.CompilerParams(
        dimension_semantics=("arbitrary",) * count, vmem_limit_bytes=vmem_bytes
    )


def cost(flops, moved):
    return pl.CostEstimate(flops=int(flops), bytes_accessed=int(moved), transcendentals=0)


def hbm(shape):
    return pltpu.HBM(shape, jnp.float32)


def in_hbm(array):
    return pltpu.with_memory_space_constraint(array, pltpu.HBM)


group_bytes = 2 * 32 * 32 * 256 * 4


def call_z_forward(phi, table):
    return pl.pallas_call(
        z_forward,
        in_specs=[anywhere, anywhere],
        out_specs=[anywhere, anywhere],
        out_shape=[hbm((128, 2 * groups, 16, 128)), hbm((32, 32, 256))],
        scratch_shapes=[
            pltpu.VMEM(table.shape, jnp.bfloat16),
            pltpu.VMEM((2 * groups, 2, 2, 32, 24, 128), jnp.float32),
            pltpu.VMEM((2 * groups, 128, 3, 8, 128), jnp.float32),
            pltpu.VMEM((32, 32, 256), jnp.float32),
            pltpu.SemaphoreType.DMA((5, 2 * groups)),
        ],
        compiler_params=pltpu.CompilerParams(vmem_limit_bytes=vmem_bytes),
        cost_estimate=cost(2.4e9, 2 * groups * group_bytes),
        name="z_forward",
    )(table, in_hbm(phi))


def call_local(phi, own, partner):
    return pl.pallas_call(
        local_part,
        grid=(groups, 4),
        in_specs=[
            pl.BlockSpec((2, 32, 8, 256), lambda g, j: (g, 0, j, 0)),
            pl.BlockSpec((32, 8, 256), lambda g, j: (0, j, 0)),
            pl.BlockSpec((32, 8, 256), lambda g, j: (0, j, 0)),
        ],
        out_specs=pl.BlockSpec((2, 32, 8, 256), lambda g, j: (g, 0, j, 0)),
        out_shape=hbm(phi.shape),
        compiler_params=params(2),
        cost_estimate=cost(50e6, 3 * groups * group_bytes),
        name="local_part",
    )(in_hbm(phi), in_hbm(own), in_hbm(partner))


anywhere = pl.BlockSpec(memory_space=pl.ANY)
inside = pl.BlockSpec(memory_space=pltpu.VMEM)


def call_middle(coefs, spec, tables):
    shapes = [
        *[pltpu.VMEM(table.shape, jnp.bfloat16) for table in tables],
        pltpu.SMEM(coefs.shape, jnp.float32),
        pltpu.VMEM((4 * groups, 256, 512), jnp.float32),
        [pltpu.VMEM((2, 512, 512), jnp.bfloat16)] * 2,
        [pltpu.VMEM((2, 512, 256), jnp.float32)] * 2,
        pltpu.VMEM((2 * groups, 64, 2, 16, 128), jnp.float32),
        pltpu.SemaphoreType.DMA((2, 2 * groups)),
    ]
    return pl.pallas_call(
        middle,
        in_specs=[anywhere, inside] + [anywhere] * len(tables),
        out_specs=anywhere,
        out_shape=hbm(spec.shape),
        scratch_shapes=shapes,
        compiler_params=pltpu.CompilerParams(vmem_limit_bytes=vmem_bytes),
        cost_estimate=cost(20e9, 6 * groups * group_bytes),
        name="middle",
    )(coefs, pltpu.with_memory_space_constraint(spec, pltpu.VMEM), *tables)


def call_z_back(spec, base, table):
    return pl.pallas_call(
        z_back,
        in_specs=[anywhere, anywhere, anywhere],
        out_specs=anywhere,
        out_shape=hbm(base.shape),
        scratch_shapes=[
            pltpu.VMEM(table.shape, jnp.bfloat16),
            pltpu.VMEM((2 * groups, 128, 3, 8, 128), jnp.float32),
            pltpu.VMEM((2 * groups, 2, 2, 32, 24, 128), jnp.float32),
            pltpu.SemaphoreType.DMA((6, 2 * groups)),
        ],
        compiler_params=pltpu.CompilerParams(vmem_limit_bytes=vmem_bytes),
        cost_estimate=cost(2.4e9, 3 * groups * group_bytes),
        name="z_back",
    )(table, spec, in_hbm(base))


def exchange(block):
    return lax.all_to_all(block, every, split_axis=0, concat_axis=0, tiled=True)


def coefficients(strains, variant_strain, variants):
    bank_rows = strains.shape[0]
    picked = variant_strain[:variants]
    one_hot = (picked[:, None] == jnp.arange(bank_rows, dtype=jnp.int32)[None, :]).astype(
        jnp.float32
    )
    chosen = jnp.dot(one_hot, strains, precision=highest)
    trace = lame_first * (chosen[:, 0] + chosen[:, 1] + chosen[:, 2])
    diagonal = jnp.asarray([1.0, 1.0, 1.0, 0.0, 0.0, 0.0], jnp.float32)
    stress = trace[:, None] * diagonal[None, :] + 2.0 * shear_mod * chosen
    plane = lax.axis_index(every).astype(jnp.float32)
    last = jnp.full((1, 12), plane, jnp.float32)
    return jnp.concatenate([jnp.concatenate([chosen, stress], axis=1), last], axis=0)


def shards(order_field, strains, variant_strain):
    length = order_field.shape[3]
    tables = [in_hbm(jnp.asarray(table)) for table in dft_tables(length)]
    z_fwd, z_inv, y_fwd, y_inv, x_fwd, x_inv = tables
    coefs = coefficients(strains, variant_strain, 12)
    sent, squares = call_z_forward(order_field, z_fwd)
    arrived = exchange(sent)
    squares, arrived = lax.optimization_barrier((squares, arrived))
    partner = lax.ppermute(squares, "var", [(0, 1), (1, 0)])
    sent = call_middle(coefs, arrived, (y_fwd, x_fwd, x_inv, y_inv))
    sent, partner = lax.optimization_barrier((sent, partner))
    returned = exchange(sent)
    base = call_local(order_field, squares, partner)
    return call_z_back(returned, base, z_inv)


def solution(mesh):
    placed = (P("var", "py", "pz", None), P(), P())
    return jax.shard_map(
        shards, mesh=mesh, in_specs=placed, out_specs=P("var", "py", "pz", None), check_vma=False
    )
```

```python
import functools

import jax
import jax.numpy as jnp
import ml_dtypes
import numpy as np
from jax import lax
from jax.experimental import pallas as pl
from jax.experimental.pallas import tpu as pltpu
from jax.sharding import PartitionSpec as P

lame_first = 1.5
shear_mod = 1.0
relax_coef = 1.0 / 1.4
grad_coef = 0.5
mobility = 0.2
landau_cubic = 3.0
landau_quartic = 0.5
two_pi = 6.283185307179586
highest = lax.Precision.HIGHEST
every = ("var", "pz", "py")
vmem_bytes = 36 * 1024 * 1024

groups = 3


def split_table(table):
    high = table.astype(ml_dtypes.bfloat16)
    low = (table - high.astype(np.float64)).astype(ml_dtypes.bfloat16)
    return high, low


def left_table(table):
    return np.concatenate(split_table(table), axis=1)


def right_table(table):
    return np.concatenate(split_table(table), axis=0)


def complex_blocks(angles, sign):
    cos, sin = np.cos(angles), sign * np.sin(angles)
    table = np.empty((2, angles.shape[0], 2, angles.shape[1]))
    table[0, :, 0], table[0, :, 1] = cos, sin
    table[1, :, 0], table[1, :, 1] = -sin, cos
    return table


@functools.cache
def dft_tables(length):
    half = length // 2
    ids = np.arange(length)
    unit = 2.0 * np.pi / length
    angles = (ids[:, None] * ids[None, :] % length) * unit
    cos, sin = np.cos(angles), np.sin(angles)
    z_fwd = left_table(np.concatenate([cos[:half], -sin[:half]], axis=0))
    weight = -mobility * np.where(np.arange(half) == 0, 1.0, 2.0)[:, None]
    z_back = right_table(np.concatenate([cos[:half] * weight, -sin[:half] * weight], axis=0))
    low = np.arange(half)
    blocks = 8
    width = length // blocks
    y_fwd, y_back, x_fwd, x_back = [], [], [], []
    for parity in range(2):
        y_ids = 2 * low + parity
        fwd = complex_blocks((y_ids[:, None] * low[None, :] % length) * unit, -1.0)
        fwd = fwd.reshape(2, blocks, width // 2, length)
        y_fwd.append(left_table(fwd.transpose(3, 1, 0, 2).reshape(length, length)))
        back = complex_blocks((low[:, None] * y_ids[None, :] % length) * unit, 1.0)
        back = back.reshape(length, 2, blocks, width // 2)
        y_back.append(left_table(back.transpose(2, 1, 3, 0).reshape(length, length)))
        x_ids = low.reshape(2, 2, width).transpose(1, 0, 2).reshape(half)
        k_ids = 2 * low + parity
        fwd = complex_blocks((x_ids[:, None] * k_ids[None, :] % length) * unit, -1.0)
        x_fwd.append(right_table(fwd.reshape(length, length)))
        back = complex_blocks((k_ids[:, None] * x_ids[None, :] % length) * unit, 1.0)
        x_back.append(right_table(back.reshape(length, length)))
    return z_fwd, z_back, np.stack(y_fwd), np.stack(y_back), np.stack(x_fwd), np.stack(x_back)


def split_value(value):
    high = value.astype(jnp.bfloat16)
    low = (value - high.astype(jnp.float32)).astype(jnp.bfloat16)
    return high, low


def as_left(value):
    high, low = split_value(value)
    return jnp.concatenate([high, low, high], axis=1)


def as_right_tr(value):
    high, low = split_value(value)
    return jnp.concatenate([high, high, low], axis=1)


def as_right(value):
    high, low = split_value(value)
    return jnp.concatenate([high, high, low], axis=0)


def left_rows(table):
    width = table.shape[1] // 2
    return jnp.concatenate([table, table[:, :width]], axis=1)


def right_rows(table):
    depth = table.shape[0] // 2
    return jnp.concatenate([table[:depth], table], axis=0)


def matmul(left, right):
    return lax.dot_general(
        left, right, (((1,), (0,)), ((), ())), preferred_element_type=jnp.float32
    )


def matmul_tr(left, right):
    return lax.dot_general(
        left, right, (((1,), (1,)), ((), ())), preferred_element_type=jnp.float32
    )


def lane_ids(rows):
    return lax.broadcasted_iota(jnp.int32, (rows, 128), 1)


def z_pieces(spec_hbm, spec_ref, grid_hbm, grid_ref, sems):
    def spec(step, back):
        group, part = step // 2 * 2, pl.multiple_of(step % 2 * 8, 8)
        place = (slice(None), pl.ds(group, 2), pl.ds(part, 8))
        ends = [spec_hbm.at[place], spec_ref.at[step, :, pl.ds(0, 2)]]
        return pltpu.make_async_copy(*(ends[::-1] if back else ends), sems.at[0, step])

    def grid(step, side, back):
        group, part = step // 2 * 2, pl.multiple_of(step % 2 * 16, 16)
        place = (pl.ds(group, 2), slice(None), pl.ds(part, 16))
        ends = [
            grid_hbm.at[place + (pl.ds(side * 128, 128),)],
            grid_ref.at[step, side, :, :, pl.ds(0, 16)],
        ]
        number = (2 if back else 0) + 1 + side
        return pltpu.make_async_copy(*(ends[::-1] if back else ends), sems.at[number, step])

    return spec, grid


def z_forward(table_hbm, phi_hbm, out_hbm, table_ref, phi_ref, out_ref, sems):
    spec, grid = z_pieces(out_hbm, out_ref, phi_hbm, phi_ref, sems)
    steps = groups * 2
    table = pltpu.make_async_copy(table_hbm, table_ref, sems.at[4, 0])
    table.start()
    for step in range(steps):
        for side in range(2):
            grid(step, side, False).start()
    table.wait()
    rows_ref = phi_ref.reshape(steps * 3072, 128)
    flat_ref = out_ref.reshape(steps * 3072, 128)

    def body(step, carry):
        for side in range(2):
            grid(step, side, False).wait()
        base = pl.multiple_of(step * 3072, 8)
        for batch in range(4):
            block = jnp.concatenate(
                [
                    jnp.concatenate(
                        [
                            rows_ref[pl.ds(base + side * 1536 + batch * 4 + y, 64, stride=24), :]
                            for side in range(2)
                        ],
                        axis=1,
                    )
                    for y in range(4)
                ],
                axis=0,
            )
            spectrum = matmul_tr(left_rows(table_ref[...]), as_right_tr(block))
            for pair in range(2):
                for part in range(2):
                    start = base + part * 8 + batch * 2 + pair
                    flat_ref[pl.ds(start, 128, stride=24), :] = spectrum[
                        part * 128 : part * 128 + 128, pair * 128 : pair * 128 + 128
                    ]
        spec(step, True).start()
        return carry

    lax.fori_loop(0, steps, body, 0)
    for step in range(steps):
        spec(step, True).wait()


def y_there(in_ref, y_ref, left_ref, ready=lambda: None):
    lanes = lane_ids(256)
    low_half = lanes < 64
    first_bit = lane_ids(128) // 32 % 2 == 0
    halves = []
    for pp in range(2):
        evens, odds = [], []
        for place in (pp, pp + 2):
            first, second = [
                jnp.concatenate(
                    [in_ref[pz * 8 + place * 2 + side].reshape(32, 128) for pz in range(8)], axis=0
                )
                for side in range(2)
            ]
            evens.append(jnp.where(low_half, first, pltpu.roll(second, 64, 1)))
            odds.append(jnp.where(low_half, pltpu.roll(first, 64, 1), second))
        rights = [as_right(jnp.concatenate(pieces, axis=1)) for pieces in (evens, odds)]
        if pp == 0:
            ready()
        even, odd = [matmul(left_rows(y_ref[side]), rights[side]) for side in range(2)]
        low, high = even + odd, even - odd
        halves.append(
            [
                [side[:, :128] + side[:, 128:], side[:, :128] - side[:, 128:]]
                for side in (low, high)
            ]
        )
    for parity in range(2):
        for side in range(2):
            for part in range(2):
                rows = slice(part * 128, part * 128 + 128)
                zero = halves[0][side][parity][rows]
                one = halves[1][side][parity][rows]
                values = (
                    jnp.where(first_bit, zero, pltpu.roll(one, 32, 1)),
                    jnp.where(first_bit, pltpu.roll(zero, 96, 1), one),
                )
                for v, value in enumerate(values):
                    high, low = split_value(value)
                    start = v * 256 + side * 128
                    for place, piece in enumerate((high, low)):
                        column = place * 256 + part * 128
                        left_ref[parity, start : start + 128, column : column + 128] = piece


def x_there(left_ref, x_ref, out_ref):
    for parity in range(2):
        product = matmul(left_rows(left_ref[parity]), right_rows(x_ref[parity]))
        for v in range(2):
            out_ref[v, :, parity * 256 : parity * 256 + 256] = product[v * 256 : v * 256 + 256]


def x_back(in_ref, x_ref, mid_ref):
    products = []
    for parity in range(2):
        columns = slice(parity * 256, parity * 256 + 256)
        block = jnp.concatenate([in_ref[0, :, columns], in_ref[1, :, columns]], axis=0)
        products.append(matmul(as_left(block), right_rows(x_ref[parity])))
    mid_ref[0] = products[0] + products[1]
    mid_ref[1] = products[0] - products[1]


def y_back(mid_ref, y_ref, out_ref):
    lanes = lane_ids(256)
    low_half = lanes < 64
    first_bit = lanes // 32 % 2 == 0
    for side in range(2):
        evens, odds = ([], []), ([], [])
        for part in range(2):
            zero = mid_ref[side, :256, part * 128 : part * 128 + 128]
            one = mid_ref[side, 256:, part * 128 : part * 128 + 128]
            merged = (
                jnp.where(first_bit, zero, pltpu.roll(one, 32, 1)),
                jnp.where(first_bit, pltpu.roll(zero, 96, 1), one),
            )
            for pp in range(2):
                evens[pp].append(merged[pp][:128] + merged[pp][128:])
                odds[pp].append(merged[pp][:128] - merged[pp][128:])
        results = []
        for parity, pieces in enumerate((evens, odds)):
            right = jnp.concatenate([jnp.concatenate(p, axis=0) for p in pieces], axis=1)
            results.append(matmul(left_rows(y_ref[parity]), as_right(right)))
        for pp in range(2):
            even = results[0][:, pp * 128 : pp * 128 + 128]
            odd = results[1][:, pp * 128 : pp * 128 + 128]
            place = (side * 2 + pp) * 2
            first = jnp.where(low_half, even, pltpu.roll(odd, 64, 1))
            second = jnp.where(low_half, pltpu.roll(even, 64, 1), odd)
            for pz in range(8):
                rows = slice(pz * 32, pz * 32 + 32)
                out_ref[pz * 8 + place] = first[rows].reshape(2, 16, 128)
                out_ref[pz * 8 + place + 1] = second[rows].reshape(2, 16, 128)


def signed_index(indices, length):
    half = length // 2
    return jnp.where(indices >= half, indices - length, indices).astype(jnp.float32)


def waves_x(wave_z, length):
    half = length // 2
    column = lax.broadcasted_iota(jnp.int32, (8, length), 1)
    kx = jnp.where(column >= half, column * 2 - (length - 1), column * 2)
    wx = signed_index(kx, length)
    keep = jnp.where(kx == half, 0.0, 1.0 / float(length * length * length))
    return wx, wx * wx + wave_z * wave_z, keep


def waves_y(row, length):
    ky = lax.broadcasted_iota(jnp.int32, (8, length), 0) + row
    return signed_index(ky, length), jnp.where(ky == length // 2, 0.0, 1.0)


def pick(value, part):
    half = value.shape[1] // 4
    return jnp.concatenate(
        [value[:, c * half : (c + 1) * half] for c in (part, part + 2)], axis=1
    )


def join(real, imag):
    half = real.shape[1] // 2
    pieces = [real[:, :half], imag[:, :half], real[:, half:], imag[:, half:]]
    return jnp.concatenate(pieces, axis=1)


def driving(strain, wx, wy, wz, squared, keep):
    inverse = 1.0 / jnp.maximum(squared, 1.0)
    trace = lame_first * (strain[0] + strain[1] + strain[2])
    s11 = trace + 2.0 * shear_mod * strain[0]
    s22 = trace + 2.0 * shear_mod * strain[1]
    s33 = trace + 2.0 * shear_mod * strain[2]
    s23 = 2.0 * shear_mod * strain[3]
    s13 = 2.0 * shear_mod * strain[4]
    s12 = 2.0 * shear_mod * strain[5]
    t1 = (s11 * wx + s12 * wy + s13 * wz) * inverse
    t2 = (s12 * wx + s22 * wy + s23 * wz) * inverse
    t3 = (s13 * wx + s23 * wy + s33 * wz) * inverse
    normal = (wx * t1 + wy * t2 + wz * t3) * (relax_coef * inverse)
    u1 = t1 - normal * wx
    u2 = t2 - normal * wy
    u3 = t3 - normal * wz
    return [
        keep * (strain[0] - wx * u1),
        keep * (strain[1] - wy * u2),
        keep * (strain[2] - wz * u3),
        keep * (2.0 * strain[3] - (wy * u3 + wz * u2)),
        keep * (2.0 * strain[4] - (wx * u3 + wz * u1)),
        keep * (2.0 * strain[5] - (wx * u2 + wy * u1)),
    ]


def middle(coef_hbm, in_ref, yf_hbm, xf_hbm, xb_hbm, yb_hbm, out_hbm, *scratch):
    yf_ref, xf_ref, xb_ref, yb_ref, coef_ref, field_ref, lefts, mids, out_ref, sems = scratch
    length = field_ref.shape[1]
    steps = groups * 2

    def part_of(ref, step):
        return ref.at[
            pl.ds(step % 2 * 64, 64),
            pl.ds(step // 2 * 2, 2),
        ]

    def departure(step):
        return pltpu.make_async_copy(out_ref.at[step], part_of(out_hbm, step), sems.at[1, step])

    def fields_of(step):
        return field_ref.at[pl.ds(step * 2, 2)]

    moves = [(yf_hbm, yf_ref), (xf_hbm, xf_ref), (xb_hbm, xb_ref), (yb_hbm, yb_ref)]
    moves.append((coef_hbm, coef_ref))
    copies = [
        pltpu.make_async_copy(source, target, sems.at[0, number])
        for number, (source, target) in enumerate(moves)
    ]
    for copy in copies:
        copy.start()

    def there_first(step, slot):
        ready = copies[0].wait if isinstance(step, int) and step == 0 else lambda: None
        y_there(part_of(in_ref, step), yf_ref, lefts[slot], ready)

    def there_second(step, slot):
        x_there(lefts[slot], xf_ref, fields_of(step))

    there_first(0, 0)
    copies[1].wait()

    def there(turn, carry):
        for slot in range(2):
            there_first(turn * 2 + slot + 1, 1 - slot)
            there_second(turn * 2 + slot, slot)
        return carry

    lax.fori_loop(0, groups - 1, there, 0)
    there_first(steps - 1, 1)
    there_second(steps - 2, 0)
    there_second(steps - 1, 1)
    copies[4].wait()
    wave_z = coef_ref[12, 0]
    places = [(p % 6 // 2 * 2 + p // 6) * 2 + p % 2 for p in range(12)]

    wx, squared_xz, keep_x = waves_x(wave_z, length)

    def tile(step, carry):
        row = pl.multiple_of(step * 8, 8)
        rows = pl.ds(row, 8)
        wy, keep_y = waves_y(row, length)
        squared = squared_xz + wy * wy
        keep = keep_x * keep_y
        half_grad = keep * squared * (grad_coef * (two_pi / length) ** 2)
        grad = join(half_grad, half_grad)
        strains = None
        for q, place in enumerate(places):
            value = field_ref[place, rows, :]
            terms = [coef_ref[q, m] * value for m in range(6)]
            strains = terms if q == 0 else [total + term for total, term in zip(strains, terms)]
        parts = [
            driving([pick(total, part) for total in strains], wx, wy, wave_z, squared, keep)
            for part in range(2)
        ]
        drive = [join(parts[0][m], parts[1][m]) for m in range(6)]
        for p, place in enumerate(places):
            total = grad * field_ref[place, rows, :]
            for m in range(6):
                total = total + coef_ref[p, 6 + m] * drive[m]
            field_ref[place, rows, :] = total
        return carry

    lax.fori_loop(0, length // 8, tile, 0)
    copies[2].wait()
    copies[3].wait()

    def back_first(step, slot):
        x_back(fields_of(step), xb_ref, mids[slot])

    def back_second(step, slot):
        y_back(mids[slot], yb_ref, out_ref.at[step])
        departure(step).start()

    back_first(0, 0)

    def back(turn, carry):
        for slot in range(2):
            back_first(turn * 2 + slot + 1, 1 - slot)
            back_second(turn * 2 + slot, slot)
        return carry

    lax.fori_loop(0, groups - 1, back, 0)
    back_first(steps - 1, 1)
    back_second(steps - 2, 0)
    back_second(steps - 1, 1)
    for step in range(steps):
        departure(step).wait()


def squares(phi_ref, out_ref):
    total = phi_ref[0] * phi_ref[0]
    for v in range(1, 2 * groups):
        total = total + phi_ref[v] * phi_ref[v]
    out_ref[...] = total


def local_part(phi_ref, own_ref, partner_ref, out_ref):
    phi = phi_ref[...]
    total_sq = own_ref[...] + partner_ref[...]
    chemical = phi - landau_cubic * phi * phi + landau_quartic * phi * total_sq[None]
    out_ref[...] = phi - mobility * chemical


def z_back(table_hbm, spec_hbm, base_hbm, out_hbm, table_ref, spec_ref, base_ref, sems):
    spec, grid = z_pieces(spec_hbm, spec_ref, base_hbm, base_ref, sems)
    grid_out = z_pieces(spec_hbm, spec_ref, out_hbm, base_ref, sems)[1]
    steps = groups * 2
    table = pltpu.make_async_copy(table_hbm, table_ref, sems.at[5, 0])
    for step in range(steps):
        spec(step, False).start()
        for side in range(2):
            grid(step, side, False).start()
        if step == 0:
            table.start()
    table.wait()
    flat_ref = spec_ref.reshape(steps * 3072, 128)
    rows_ref = base_ref.reshape(steps * 3072, 128)

    def body(step, carry):
        base = pl.multiple_of(step * 3072, 8)
        spec(step, False).wait()
        for side in range(2):
            grid(step, side, False).wait()
        for batch in range(4):
            lefts = []
            for pair in range(2):
                turned = []
                for part in range(2):
                    start = base + part * 8 + batch * 2 + pair
                    turned.append(flat_ref[pl.ds(start, 128, stride=24), :].T)
                lefts.append(jnp.concatenate(turned, axis=1))
            force = matmul(as_left(jnp.concatenate(lefts, axis=0)), right_rows(table_ref[...]))
            for y in range(4):
                for side in range(2):
                    rows = pl.ds(base + side * 1536 + batch * 4 + y, 64, stride=24)
                    lanes = slice(side * 128, side * 128 + 128)
                    rows_ref[rows, :] = rows_ref[rows, :] + force[y * 64 : y * 64 + 64, lanes]
        for side in range(2):
            grid_out(step, side, True).start()
        return carry

    lax.fori_loop(0, steps, body, 0)
    for step in range(steps):
        for side in range(2):
            grid_out(step, side, True).wait()


def params(count):
    return pltpu.CompilerParams(
        dimension_semantics=("arbitrary",) * count, vmem_limit_bytes=vmem_bytes
    )


def cost(flops, moved):
    return pl.CostEstimate(flops=int(flops), bytes_accessed=int(moved), transcendentals=0)


def hbm(shape):
    return pltpu.HBM(shape, jnp.float32)


def in_hbm(array):
    return pltpu.with_memory_space_constraint(array, pltpu.HBM)


group_bytes = 2 * 32 * 32 * 256 * 4


def call_z_forward(phi, table):
    return pl.pallas_call(
        z_forward,
        in_specs=[anywhere, anywhere],
        out_specs=anywhere,
        out_shape=hbm((128, 2 * groups, 16, 128)),
        scratch_shapes=[
            pltpu.VMEM(table.shape, jnp.bfloat16),
            pltpu.VMEM((2 * groups, 2, 2, 32, 24, 128), jnp.float32),
            pltpu.VMEM((2 * groups, 128, 3, 8, 128), jnp.float32),
            pltpu.SemaphoreType.DMA((5, 2 * groups)),
        ],
        compiler_params=pltpu.CompilerParams(vmem_limit_bytes=vmem_bytes),
        cost_estimate=cost(2.4e9, 2 * groups * group_bytes),
        name="z_forward",
    )(table, in_hbm(phi))


def call_squares(phi):
    return pl.pallas_call(
        squares,
        grid=(4,),
        in_specs=[pl.BlockSpec((2 * groups, 32, 8, 256), lambda j: (0, 0, j, 0))],
        out_specs=pl.BlockSpec((32, 8, 256), lambda j: (0, j, 0)),
        out_shape=hbm((32, 32, 256)),
        compiler_params=params(1),
        cost_estimate=cost(20e6, groups * group_bytes),
        name="squares",
    )(in_hbm(phi))


def call_local(phi, own, partner):
    return pl.pallas_call(
        local_part,
        grid=(groups, 4),
        in_specs=[
            pl.BlockSpec((2, 32, 8, 256), lambda g, j: (g, 0, j, 0)),
            pl.BlockSpec((32, 8, 256), lambda g, j: (0, j, 0)),
            pl.BlockSpec((32, 8, 256), lambda g, j: (0, j, 0)),
        ],
        out_specs=pl.BlockSpec((2, 32, 8, 256), lambda g, j: (g, 0, j, 0)),
        out_shape=hbm(phi.shape),
        compiler_params=params(2),
        cost_estimate=cost(50e6, 3 * groups * group_bytes),
        name="local_part",
    )(in_hbm(phi), in_hbm(own), partner)


anywhere = pl.BlockSpec(memory_space=pl.ANY)
inside = pl.BlockSpec(memory_space=pltpu.VMEM)


def call_middle(coefs, spec, tables):
    shapes = [
        *[pltpu.VMEM(table.shape, jnp.bfloat16) for table in tables],
        pltpu.SMEM(coefs.shape, jnp.float32),
        pltpu.VMEM((4 * groups, 256, 512), jnp.float32),
        [pltpu.VMEM((2, 512, 512), jnp.bfloat16)] * 2,
        [pltpu.VMEM((2, 512, 256), jnp.float32)] * 2,
        pltpu.VMEM((2 * groups, 64, 2, 16, 128), jnp.float32),
        pltpu.SemaphoreType.DMA((2, 2 * groups)),
    ]
    return pl.pallas_call(
        middle,
        in_specs=[anywhere, inside] + [anywhere] * len(tables),
        out_specs=anywhere,
        out_shape=hbm(spec.shape),
        scratch_shapes=shapes,
        compiler_params=pltpu.CompilerParams(vmem_limit_bytes=vmem_bytes),
        cost_estimate=cost(20e9, 6 * groups * group_bytes),
        name="middle",
    )(coefs, pltpu.with_memory_space_constraint(spec, pltpu.VMEM), *tables)


def call_z_back(spec, base, table):
    return pl.pallas_call(
        z_back,
        in_specs=[anywhere, anywhere, anywhere],
        out_specs=anywhere,
        out_shape=hbm(base.shape),
        scratch_shapes=[
            pltpu.VMEM(table.shape, jnp.bfloat16),
            pltpu.VMEM((2 * groups, 128, 3, 8, 128), jnp.float32),
            pltpu.VMEM((2 * groups, 2, 2, 32, 24, 128), jnp.float32),
            pltpu.SemaphoreType.DMA((6, 2 * groups)),
        ],
        compiler_params=pltpu.CompilerParams(vmem_limit_bytes=vmem_bytes),
        cost_estimate=cost(2.4e9, 3 * groups * group_bytes),
        name="z_back",
    )(table, spec, in_hbm(base))


def exchange(block):
    return lax.all_to_all(block, every, split_axis=0, concat_axis=0, tiled=True)


def coefficients(strains, variant_strain, variants):
    bank_rows = strains.shape[0]
    picked = variant_strain[:variants]
    one_hot = (picked[:, None] == jnp.arange(bank_rows, dtype=jnp.int32)[None, :]).astype(
        jnp.float32
    )
    chosen = jnp.dot(one_hot, strains, precision=highest)
    trace = lame_first * (chosen[:, 0] + chosen[:, 1] + chosen[:, 2])
    diagonal = jnp.asarray([1.0, 1.0, 1.0, 0.0, 0.0, 0.0], jnp.float32)
    stress = trace[:, None] * diagonal[None, :] + 2.0 * shear_mod * chosen
    plane = lax.axis_index(every).astype(jnp.float32)
    last = jnp.full((1, 12), plane, jnp.float32)
    return jnp.concatenate([jnp.concatenate([chosen, stress], axis=1), last], axis=0)


def shards(order_field, strains, variant_strain):
    length = order_field.shape[3]
    tables = [in_hbm(jnp.asarray(table)) for table in dft_tables(length)]
    z_fwd, z_inv, y_fwd, y_inv, x_fwd, x_inv = tables
    coefs = coefficients(strains, variant_strain, 12)
    sent, later_field = lax.optimization_barrier((call_z_forward(order_field, z_fwd), order_field))
    arrived = exchange(sent)
    own = call_squares(later_field)
    own, arrived = lax.optimization_barrier((own, arrived))
    partner = lax.ppermute(own, "var", [(0, 1), (1, 0)])
    sent = call_middle(coefs, arrived, (y_fwd, x_fwd, x_inv, y_inv))
    sent, partner = lax.optimization_barrier((sent, partner))
    returned = exchange(sent)
    base = call_local(order_field, own, partner)
    return call_z_back(returned, base, z_inv)


def solution(mesh):
    placed = (P("var", "py", "pz", None), P(), P())
    return jax.shard_map(
        shards, mesh=mesh, in_specs=placed, out_specs=P("var", "py", "pz", None), check_vma=False
    )
```

```python
import functools

import jax
import jax.numpy as jnp
import ml_dtypes
import numpy as np
from jax import lax
from jax.experimental import pallas as pl
from jax.experimental.pallas import tpu as pltpu
from jax.sharding import PartitionSpec as P

lame_first = 1.5
shear_mod = 1.0
relax_coef = 1.0 / 1.4
grad_coef = 0.5
mobility = 0.2
landau_cubic = 3.0
landau_quartic = 0.5
two_pi = 6.283185307179586
highest = lax.Precision.HIGHEST
every = ("var", "pz", "py")
vmem_bytes = 36 * 1024 * 1024

groups = 3


def split_table(table):
    high = table.astype(ml_dtypes.bfloat16)
    low = (table - high.astype(np.float64)).astype(ml_dtypes.bfloat16)
    return high, low


def left_table(table):
    return np.concatenate(split_table(table), axis=1)


def right_table(table):
    return np.concatenate(split_table(table), axis=0)


def complex_blocks(angles, sign):
    cos, sin = np.cos(angles), sign * np.sin(angles)
    table = np.empty((2, angles.shape[0], 2, angles.shape[1]))
    table[0, :, 0], table[0, :, 1] = cos, sin
    table[1, :, 0], table[1, :, 1] = -sin, cos
    return table


@functools.cache
def dft_tables(length):
    half = length // 2
    ids = np.arange(length)
    unit = 2.0 * np.pi / length
    angles = (ids[:, None] * ids[None, :] % length) * unit
    cos, sin = np.cos(angles), np.sin(angles)
    z_fwd = left_table(np.concatenate([cos[:half], -sin[:half]], axis=0))
    weight = -mobility * np.where(np.arange(half) == 0, 1.0, 2.0)[:, None]
    z_back = right_table(np.concatenate([cos[:half] * weight, -sin[:half] * weight], axis=0))
    low = np.arange(half)
    blocks = 8
    width = length // blocks
    y_fwd, y_back, x_fwd, x_back = [], [], [], []
    for parity in range(2):
        y_ids = 2 * low + parity
        fwd = complex_blocks((y_ids[:, None] * low[None, :] % length) * unit, -1.0)
        fwd = fwd.reshape(2, blocks, width // 2, length)
        y_fwd.append(left_table(fwd.transpose(3, 1, 0, 2).reshape(length, length)))
        back = complex_blocks((low[:, None] * y_ids[None, :] % length) * unit, 1.0)
        back = back.reshape(length, 2, blocks, width // 2)
        y_back.append(left_table(back.transpose(2, 1, 3, 0).reshape(length, length)))
        x_ids = low.reshape(2, 2, width).transpose(1, 0, 2).reshape(half)
        k_ids = 2 * low + parity
        fwd = complex_blocks((x_ids[:, None] * k_ids[None, :] % length) * unit, -1.0)
        x_fwd.append(right_table(fwd.reshape(length, length)))
        back = complex_blocks((k_ids[:, None] * x_ids[None, :] % length) * unit, 1.0)
        x_back.append(right_table(back.reshape(length, length)))
    return z_fwd, z_back, np.stack(y_fwd), np.stack(y_back), np.stack(x_fwd), np.stack(x_back)


def split_value(value):
    high = value.astype(jnp.bfloat16)
    low = (value - high.astype(jnp.float32)).astype(jnp.bfloat16)
    return high, low


def as_left(value):
    high, low = split_value(value)
    return jnp.concatenate([high, low, high], axis=1)


def as_right_tr(value):
    high, low = split_value(value)
    return jnp.concatenate([high, high, low], axis=1)


def as_right(value):
    high, low = split_value(value)
    return jnp.concatenate([high, high, low], axis=0)


def left_rows(table):
    width = table.shape[1] // 2
    return jnp.concatenate([table, table[:, :width]], axis=1)


def right_rows(table):
    depth = table.shape[0] // 2
    return jnp.concatenate([table[:depth], table], axis=0)


def matmul(left, right):
    return lax.dot_general(
        left, right, (((1,), (0,)), ((), ())), preferred_element_type=jnp.float32
    )


def matmul_tr(left, right):
    return lax.dot_general(
        left, right, (((1,), (1,)), ((), ())), preferred_element_type=jnp.float32
    )


def lane_ids(rows):
    return lax.broadcasted_iota(jnp.int32, (rows, 128), 1)


def z_pieces(spec_hbm, spec_ref, grid_hbm, grid_ref, sems):
    def spec(step, back):
        group, part = step // 2 * 2, pl.multiple_of(step % 2 * 8, 8)
        place = (slice(None), pl.ds(group, 2), pl.ds(part, 8))
        ends = [spec_hbm.at[place], spec_ref.at[step, :, pl.ds(0, 2)]]
        return pltpu.make_async_copy(*(ends[::-1] if back else ends), sems.at[0, step])

    def grid(step, side, back):
        group, part = step // 2 * 2, pl.multiple_of(step % 2 * 16, 16)
        place = (pl.ds(group, 2), slice(None), pl.ds(part, 16))
        ends = [
            grid_hbm.at[place + (pl.ds(side * 128, 128),)],
            grid_ref.at[step, side, :, :, pl.ds(0, 16)],
        ]
        number = (2 if back else 0) + 1 + side
        return pltpu.make_async_copy(*(ends[::-1] if back else ends), sems.at[number, step])

    return spec, grid


def z_forward(table_hbm, phi_hbm, out_hbm, table_ref, phi_ref, out_ref, sems):
    spec, grid = z_pieces(out_hbm, out_ref, phi_hbm, phi_ref, sems)
    steps = groups * 2
    table = pltpu.make_async_copy(table_hbm, table_ref, sems.at[4, 0])
    table.start()
    for step in range(steps):
        for side in range(2):
            grid(step, side, False).start()
    table.wait()
    rows_ref = phi_ref.reshape((steps + 1) * 3072, 128)
    flat_ref = out_ref.reshape((steps + 1) * 3072, 128)

    def body(step, carry):
        for side in range(2):
            grid(step, side, False).wait()
        base = pl.multiple_of(step * 3072, 8)
        for batch in range(4):
            block = jnp.concatenate(
                [
                    jnp.concatenate(
                        [
                            rows_ref[pl.ds(base + side * 1536 + batch * 4 + y, 64, stride=24), :]
                            for side in range(2)
                        ],
                        axis=1,
                    )
                    for y in range(4)
                ],
                axis=0,
            )
            spectrum = matmul_tr(left_rows(table_ref[...]), as_right_tr(block))
            for pair in range(2):
                for part in range(2):
                    start = base + part * 8 + batch * 2 + pair
                    flat_ref[pl.ds(start, 128, stride=24), :] = spectrum[
                        part * 128 : part * 128 + 128, pair * 128 : pair * 128 + 128
                    ]
        spec(step, True).start()
        return carry

    lax.fori_loop(0, steps, body, 0)
    for step in range(steps):
        spec(step, True).wait()


def y_there(in_ref, y_ref, left_ref, ready=lambda: None):
    lanes = lane_ids(256)
    low_half = lanes < 64
    first_bit = lane_ids(128) // 32 % 2 == 0
    halves = []
    for pp in range(2):
        evens, odds = [], []
        for place in (pp, pp + 2):
            first, second = [
                jnp.concatenate(
                    [in_ref[pz * 8 + place * 2 + side].reshape(32, 128) for pz in range(8)], axis=0
                )
                for side in range(2)
            ]
            evens.append(jnp.where(low_half, first, pltpu.roll(second, 64, 1)))
            odds.append(jnp.where(low_half, pltpu.roll(first, 64, 1), second))
        rights = [as_right(jnp.concatenate(pieces, axis=1)) for pieces in (evens, odds)]
        if pp == 0:
            ready()
        even, odd = [matmul(left_rows(y_ref[side]), rights[side]) for side in range(2)]
        low, high = even + odd, even - odd
        halves.append(
            [
                [side[:, :128] + side[:, 128:], side[:, :128] - side[:, 128:]]
                for side in (low, high)
            ]
        )
    for parity in range(2):
        for side in range(2):
            for part in range(2):
                rows = slice(part * 128, part * 128 + 128)
                zero = halves[0][side][parity][rows]
                one = halves[1][side][parity][rows]
                values = (
                    jnp.where(first_bit, zero, pltpu.roll(one, 32, 1)),
                    jnp.where(first_bit, pltpu.roll(zero, 96, 1), one),
                )
                for v, value in enumerate(values):
                    high, low = split_value(value)
                    start = v * 256 + side * 128
                    for place, piece in enumerate((high, low)):
                        column = place * 256 + part * 128
                        left_ref[parity, start : start + 128, column : column + 128] = piece


def x_there(left_ref, x_ref, out_ref):
    for parity in range(2):
        product = matmul(left_rows(left_ref[parity]), right_rows(x_ref[parity]))
        for v in range(2):
            out_ref[v, :, parity * 256 : parity * 256 + 256] = product[v * 256 : v * 256 + 256]


def x_back(in_ref, x_ref, mid_ref):
    products = []
    for parity in range(2):
        columns = slice(parity * 256, parity * 256 + 256)
        block = jnp.concatenate([in_ref[0, :, columns], in_ref[1, :, columns]], axis=0)
        products.append(matmul(as_left(block), right_rows(x_ref[parity])))
    mid_ref[0] = products[0] + products[1]
    mid_ref[1] = products[0] - products[1]


def y_back(mid_ref, y_ref, out_ref):
    lanes = lane_ids(256)
    low_half = lanes < 64
    first_bit = lanes // 32 % 2 == 0
    for side in range(2):
        evens, odds = ([], []), ([], [])
        for part in range(2):
            zero = mid_ref[side, :256, part * 128 : part * 128 + 128]
            one = mid_ref[side, 256:, part * 128 : part * 128 + 128]
            merged = (
                jnp.where(first_bit, zero, pltpu.roll(one, 32, 1)),
                jnp.where(first_bit, pltpu.roll(zero, 96, 1), one),
            )
            for pp in range(2):
                evens[pp].append(merged[pp][:128] + merged[pp][128:])
                odds[pp].append(merged[pp][:128] - merged[pp][128:])
        results = []
        for parity, pieces in enumerate((evens, odds)):
            right = jnp.concatenate([jnp.concatenate(p, axis=0) for p in pieces], axis=1)
            results.append(matmul(left_rows(y_ref[parity]), as_right(right)))
        for pp in range(2):
            even = results[0][:, pp * 128 : pp * 128 + 128]
            odd = results[1][:, pp * 128 : pp * 128 + 128]
            place = (side * 2 + pp) * 2
            first = jnp.where(low_half, even, pltpu.roll(odd, 64, 1))
            second = jnp.where(low_half, pltpu.roll(even, 64, 1), odd)
            for pz in range(8):
                rows = slice(pz * 32, pz * 32 + 32)
                out_ref[pz * 8 + place] = first[rows].reshape(2, 16, 128)
                out_ref[pz * 8 + place + 1] = second[rows].reshape(2, 16, 128)


def signed_index(indices, length):
    half = length // 2
    return jnp.where(indices >= half, indices - length, indices).astype(jnp.float32)


def waves_x(wave_z, length):
    half = length // 2
    column = lax.broadcasted_iota(jnp.int32, (8, length), 1)
    kx = jnp.where(column >= half, column * 2 - (length - 1), column * 2)
    wx = signed_index(kx, length)
    keep = jnp.where(kx == half, 0.0, 1.0 / float(length * length * length))
    return wx, wx * wx + wave_z * wave_z, keep


def waves_y(row, length):
    ky = lax.broadcasted_iota(jnp.int32, (8, length), 0) + row
    return signed_index(ky, length), jnp.where(ky == length // 2, 0.0, 1.0)


def pick(value, part):
    half = value.shape[1] // 4
    return jnp.concatenate(
        [value[:, c * half : (c + 1) * half] for c in (part, part + 2)], axis=1
    )


def join(real, imag):
    half = real.shape[1] // 2
    pieces = [real[:, :half], imag[:, :half], real[:, half:], imag[:, half:]]
    return jnp.concatenate(pieces, axis=1)


def driving(strain, wx, wy, wz, squared, keep):
    inverse = 1.0 / jnp.maximum(squared, 1.0)
    trace = lame_first * (strain[0] + strain[1] + strain[2])
    s11 = trace + 2.0 * shear_mod * strain[0]
    s22 = trace + 2.0 * shear_mod * strain[1]
    s33 = trace + 2.0 * shear_mod * strain[2]
    s23 = 2.0 * shear_mod * strain[3]
    s13 = 2.0 * shear_mod * strain[4]
    s12 = 2.0 * shear_mod * strain[5]
    t1 = (s11 * wx + s12 * wy + s13 * wz) * inverse
    t2 = (s12 * wx + s22 * wy + s23 * wz) * inverse
    t3 = (s13 * wx + s23 * wy + s33 * wz) * inverse
    normal = (wx * t1 + wy * t2 + wz * t3) * (relax_coef * inverse)
    u1 = t1 - normal * wx
    u2 = t2 - normal * wy
    u3 = t3 - normal * wz
    return [
        keep * (strain[0] - wx * u1),
        keep * (strain[1] - wy * u2),
        keep * (strain[2] - wz * u3),
        keep * (2.0 * strain[3] - (wy * u3 + wz * u2)),
        keep * (2.0 * strain[4] - (wx * u3 + wz * u1)),
        keep * (2.0 * strain[5] - (wx * u2 + wy * u1)),
    ]


def middle(coef_hbm, in_ref, yf_hbm, xf_hbm, xb_hbm, yb_hbm, out_hbm, *scratch):
    yf_ref, xf_ref, xb_ref, yb_ref, coef_ref, field_ref, lefts, mids, out_ref, sems = scratch
    length = field_ref.shape[1]
    steps = groups * 2

    def part_of(ref, step):
        return ref.at[
            pl.ds(step % 2 * 64, 64),
            pl.ds(step // 2 * 2, 2),
        ]

    def departure(step):
        return pltpu.make_async_copy(out_ref.at[step], part_of(out_hbm, step), sems.at[1, step])

    def fields_of(step):
        return field_ref.at[pl.ds(step * 2, 2)]

    moves = [(yf_hbm, yf_ref), (xf_hbm, xf_ref), (xb_hbm, xb_ref), (yb_hbm, yb_ref)]
    moves.append((coef_hbm, coef_ref))
    copies = [
        pltpu.make_async_copy(source, target, sems.at[0, number])
        for number, (source, target) in enumerate(moves)
    ]
    for copy in copies:
        copy.start()

    def there_first(step, slot):
        ready = copies[0].wait if isinstance(step, int) and step == 0 else lambda: None
        y_there(part_of(in_ref, step), yf_ref, lefts[slot], ready)

    def there_second(step, slot):
        x_there(lefts[slot], xf_ref, fields_of(step))

    there_first(0, 0)
    copies[1].wait()

    def there(turn, carry):
        for slot in range(2):
            there_first(turn * 2 + slot + 1, 1 - slot)
            there_second(turn * 2 + slot, slot)
        return carry

    lax.fori_loop(0, groups - 1, there, 0)
    there_first(steps - 1, 1)
    there_second(steps - 2, 0)
    there_second(steps - 1, 1)
    copies[4].wait()
    wave_z = coef_ref[12, 0]
    places = [(p % 6 // 2 * 2 + p // 6) * 2 + p % 2 for p in range(12)]

    wx, squared_xz, keep_x = waves_x(wave_z, length)

    def tile(step, carry):
        row = pl.multiple_of(step * 8, 8)
        rows = pl.ds(row, 8)
        wy, keep_y = waves_y(row, length)
        squared = squared_xz + wy * wy
        keep = keep_x * keep_y
        half_grad = keep * squared * (grad_coef * (two_pi / length) ** 2)
        grad = join(half_grad, half_grad)
        strains = None
        for q, place in enumerate(places):
            value = field_ref[place, rows, :]
            terms = [coef_ref[q, m] * value for m in range(6)]
            strains = terms if q == 0 else [total + term for total, term in zip(strains, terms)]
        parts = [
            driving([pick(total, part) for total in strains], wx, wy, wave_z, squared, keep)
            for part in range(2)
        ]
        drive = [join(parts[0][m], parts[1][m]) for m in range(6)]
        for p, place in enumerate(places):
            total = grad * field_ref[place, rows, :]
            for m in range(6):
                total = total + coef_ref[p, 6 + m] * drive[m]
            field_ref[place, rows, :] = total
        return carry

    lax.fori_loop(0, length // 8, tile, 0)
    copies[2].wait()
    copies[3].wait()

    def back_first(step, slot):
        x_back(fields_of(step), xb_ref, mids[slot])

    def back_second(step, slot):
        y_back(mids[slot], yb_ref, out_ref.at[step])
        departure(step).start()

    back_first(0, 0)

    def back(turn, carry):
        for slot in range(2):
            back_first(turn * 2 + slot + 1, 1 - slot)
            back_second(turn * 2 + slot, slot)
        return carry

    lax.fori_loop(0, groups - 1, back, 0)
    back_first(steps - 1, 1)
    back_second(steps - 2, 0)
    back_second(steps - 1, 1)
    for step in range(steps):
        departure(step).wait()


def squares(phi_ref, out_ref):
    total = phi_ref[0] * phi_ref[0]
    for v in range(1, 2 * groups):
        total = total + phi_ref[v] * phi_ref[v]
    out_ref[...] = total


def local_part(phi_ref, own_ref, partner_ref, out_ref):
    phi = phi_ref[...]
    total_sq = own_ref[...] + partner_ref[...]
    chemical = phi - landau_cubic * phi * phi + landau_quartic * phi * total_sq[None]
    out_ref[...] = phi - mobility * chemical


def z_back(table_hbm, spec_hbm, base_hbm, out_hbm, table_ref, spec_ref, base_ref, sems):
    spec, grid = z_pieces(spec_hbm, spec_ref, base_hbm, base_ref, sems)
    grid_out = z_pieces(spec_hbm, spec_ref, out_hbm, base_ref, sems)[1]
    steps = groups * 2
    table = pltpu.make_async_copy(table_hbm, table_ref, sems.at[5, 0])
    for step in range(steps):
        spec(step, False).start()
        for side in range(2):
            grid(step, side, False).start()
        if step == 0:
            table.start()
    table.wait()
    flat_ref = spec_ref.reshape((steps + 1) * 3072, 128)
    rows_ref = base_ref.reshape((steps + 1) * 3072, 128)

    def body(step, carry):
        base = pl.multiple_of(step * 3072, 8)
        spec(step, False).wait()
        for side in range(2):
            grid(step, side, False).wait()
        for batch in range(4):
            lefts = []
            for pair in range(2):
                turned = []
                for part in range(2):
                    start = base + part * 8 + batch * 2 + pair
                    turned.append(flat_ref[pl.ds(start, 128, stride=24), :].T)
                lefts.append(jnp.concatenate(turned, axis=1))
            force = matmul(as_left(jnp.concatenate(lefts, axis=0)), right_rows(table_ref[...]))
            for y in range(4):
                for side in range(2):
                    rows = pl.ds(base + side * 1536 + batch * 4 + y, 64, stride=24)
                    lanes = slice(side * 128, side * 128 + 128)
                    rows_ref[rows, :] = rows_ref[rows, :] + force[y * 64 : y * 64 + 64, lanes]
        for side in range(2):
            grid_out(step, side, True).start()
        return carry

    lax.fori_loop(0, steps, body, 0)
    for step in range(steps):
        for side in range(2):
            grid_out(step, side, True).wait()


def params(count):
    return pltpu.CompilerParams(
        dimension_semantics=("arbitrary",) * count, vmem_limit_bytes=vmem_bytes
    )


def cost(flops, moved):
    return pl.CostEstimate(flops=int(flops), bytes_accessed=int(moved), transcendentals=0)


def hbm(shape):
    return pltpu.HBM(shape, jnp.float32)


def in_hbm(array):
    return pltpu.with_memory_space_constraint(array, pltpu.HBM)


group_bytes = 2 * 32 * 32 * 256 * 4


def call_z_forward(phi, table):
    return pl.pallas_call(
        z_forward,
        in_specs=[anywhere, anywhere],
        out_specs=anywhere,
        out_shape=hbm((128, 2 * groups, 16, 128)),
        scratch_shapes=[
            pltpu.VMEM(table.shape, jnp.bfloat16),
            pltpu.VMEM((2 * groups + 1, 2, 2, 32, 24, 128), jnp.float32),
            pltpu.VMEM((2 * groups + 1, 128, 3, 8, 128), jnp.float32),
            pltpu.SemaphoreType.DMA((5, 2 * groups)),
        ],
        compiler_params=pltpu.CompilerParams(vmem_limit_bytes=vmem_bytes),
        cost_estimate=cost(2.4e9, 2 * groups * group_bytes),
        name="z_forward",
    )(table, in_hbm(phi))


def call_squares(phi):
    return pl.pallas_call(
        squares,
        grid=(4,),
        in_specs=[pl.BlockSpec((2 * groups, 32, 8, 256), lambda j: (0, 0, j, 0))],
        out_specs=pl.BlockSpec((32, 8, 256), lambda j: (0, j, 0)),
        out_shape=hbm((32, 32, 256)),
        compiler_params=params(1),
        cost_estimate=cost(20e6, groups * group_bytes),
        name="squares",
    )(in_hbm(phi))


def call_local(phi, own, partner):
    return pl.pallas_call(
        local_part,
        grid=(groups, 4),
        in_specs=[
            pl.BlockSpec((2, 32, 8, 256), lambda g, j: (g, 0, j, 0)),
            pl.BlockSpec((32, 8, 256), lambda g, j: (0, j, 0)),
            pl.BlockSpec((32, 8, 256), lambda g, j: (0, j, 0)),
        ],
        out_specs=pl.BlockSpec((2, 32, 8, 256), lambda g, j: (g, 0, j, 0)),
        out_shape=hbm(phi.shape),
        compiler_params=params(2),
        cost_estimate=cost(50e6, 3 * groups * group_bytes),
        name="local_part",
    )(in_hbm(phi), in_hbm(own), partner)


anywhere = pl.BlockSpec(memory_space=pl.ANY)
inside = pl.BlockSpec(memory_space=pltpu.VMEM)


def call_middle(coefs, spec, tables):
    shapes = [
        *[pltpu.VMEM(table.shape, jnp.bfloat16) for table in tables],
        pltpu.SMEM(coefs.shape, jnp.float32),
        pltpu.VMEM((4 * groups, 256, 512), jnp.float32),
        [pltpu.VMEM((2, 512, 512), jnp.bfloat16)] * 2,
        [pltpu.VMEM((2, 512, 256), jnp.float32)] * 2,
        pltpu.VMEM((2 * groups, 64, 2, 16, 128), jnp.float32),
        pltpu.SemaphoreType.DMA((2, 2 * groups)),
    ]
    return pl.pallas_call(
        middle,
        in_specs=[anywhere, inside] + [anywhere] * len(tables),
        out_specs=anywhere,
        out_shape=hbm(spec.shape),
        scratch_shapes=shapes,
        compiler_params=pltpu.CompilerParams(vmem_limit_bytes=vmem_bytes),
        cost_estimate=cost(20e9, 6 * groups * group_bytes),
        name="middle",
    )(coefs, pltpu.with_memory_space_constraint(spec, pltpu.VMEM), *tables)


def call_z_back(spec, base, table):
    return pl.pallas_call(
        z_back,
        in_specs=[anywhere, anywhere, anywhere],
        out_specs=anywhere,
        out_shape=hbm(base.shape),
        scratch_shapes=[
            pltpu.VMEM(table.shape, jnp.bfloat16),
            pltpu.VMEM((2 * groups + 1, 128, 3, 8, 128), jnp.float32),
            pltpu.VMEM((2 * groups + 1, 2, 2, 32, 24, 128), jnp.float32),
            pltpu.SemaphoreType.DMA((6, 2 * groups)),
        ],
        compiler_params=pltpu.CompilerParams(vmem_limit_bytes=vmem_bytes),
        cost_estimate=cost(2.4e9, 3 * groups * group_bytes),
        name="z_back",
    )(table, spec, in_hbm(base))


def exchange(block):
    return lax.all_to_all(block, every, split_axis=0, concat_axis=0, tiled=True)


def coefficients(strains, variant_strain, variants):
    bank_rows = strains.shape[0]
    picked = variant_strain[:variants]
    one_hot = (picked[:, None] == jnp.arange(bank_rows, dtype=jnp.int32)[None, :]).astype(
        jnp.float32
    )
    chosen = jnp.dot(one_hot, strains, precision=highest)
    trace = lame_first * (chosen[:, 0] + chosen[:, 1] + chosen[:, 2])
    diagonal = jnp.asarray([1.0, 1.0, 1.0, 0.0, 0.0, 0.0], jnp.float32)
    stress = trace[:, None] * diagonal[None, :] + 2.0 * shear_mod * chosen
    plane = lax.axis_index(every).astype(jnp.float32)
    last = jnp.full((1, 12), plane, jnp.float32)
    return jnp.concatenate([jnp.concatenate([chosen, stress], axis=1), last], axis=0)


def shards(order_field, strains, variant_strain):
    length = order_field.shape[3]
    tables = [in_hbm(jnp.asarray(table)) for table in dft_tables(length)]
    z_fwd, z_inv, y_fwd, y_inv, x_fwd, x_inv = tables
    coefs = coefficients(strains, variant_strain, 12)
    sent, later_field = lax.optimization_barrier((call_z_forward(order_field, z_fwd), order_field))
    arrived = exchange(sent)
    own = call_squares(later_field)
    own, arrived = lax.optimization_barrier((own, arrived))
    partner = lax.ppermute(own, "var", [(0, 1), (1, 0)])
    sent = call_middle(coefs, arrived, (y_fwd, x_fwd, x_inv, y_inv))
    sent, partner = lax.optimization_barrier((sent, partner))
    returned = exchange(sent)
    base = call_local(order_field, own, partner)
    return call_z_back(returned, base, z_inv)


def solution(mesh):
    placed = (P("var", "py", "pz", None), P(), P())
    return jax.shard_map(
        shards, mesh=mesh, in_specs=placed, out_specs=P("var", "py", "pz", None), check_vma=False
    )
```

```python
import functools

import jax
import jax.numpy as jnp
import ml_dtypes
import numpy as np
from jax import lax
from jax.experimental import pallas as pl
from jax.experimental.pallas import tpu as pltpu
from jax.sharding import PartitionSpec as P

lame_first = 1.5
shear_mod = 1.0
relax_coef = 1.0 / 1.4
grad_coef = 0.5
mobility = 0.2
landau_cubic = 3.0
landau_quartic = 0.5
two_pi = 6.283185307179586
highest = lax.Precision.HIGHEST
every = ("var", "pz", "py")
vmem_bytes = 36 * 1024 * 1024

groups = 3


def split_table(table):
    high = table.astype(ml_dtypes.bfloat16)
    low = (table - high.astype(np.float64)).astype(ml_dtypes.bfloat16)
    return high, low


def left_table(table):
    return np.concatenate(split_table(table), axis=1)


def right_table(table):
    return np.concatenate(split_table(table), axis=0)


def complex_blocks(angles, sign):
    cos, sin = np.cos(angles), sign * np.sin(angles)
    table = np.empty((2, angles.shape[0], 2, angles.shape[1]))
    table[0, :, 0], table[0, :, 1] = cos, sin
    table[1, :, 0], table[1, :, 1] = -sin, cos
    return table


@functools.cache
def dft_tables(length):
    half = length // 2
    ids = np.arange(length)
    unit = 2.0 * np.pi / length
    angles = (ids[:, None] * ids[None, :] % length) * unit
    cos, sin = np.cos(angles), np.sin(angles)
    z_fwd = left_table(np.concatenate([cos[:half], -sin[:half]], axis=0))
    weight = -mobility * np.where(np.arange(half) == 0, 1.0, 2.0)[:, None]
    z_back = right_table(np.concatenate([cos[:half] * weight, -sin[:half] * weight], axis=0))
    low = np.arange(half)
    blocks = 8
    width = length // blocks
    y_fwd, y_back, x_fwd, x_back = [], [], [], []
    for parity in range(2):
        y_ids = 2 * low + parity
        fwd = complex_blocks((y_ids[:, None] * low[None, :] % length) * unit, -1.0)
        fwd = fwd.reshape(2, blocks, width // 2, length)
        y_fwd.append(left_table(fwd.transpose(3, 1, 0, 2).reshape(length, length)))
        back = complex_blocks((low[:, None] * y_ids[None, :] % length) * unit, 1.0)
        back = back.reshape(length, 2, blocks, width // 2)
        y_back.append(left_table(back.transpose(2, 1, 3, 0).reshape(length, length)))
        x_ids = low.reshape(2, 2, width).transpose(1, 0, 2).reshape(half)
        k_ids = 2 * low + parity
        fwd = complex_blocks((x_ids[:, None] * k_ids[None, :] % length) * unit, -1.0)
        x_fwd.append(right_table(fwd.reshape(length, length)))
        back = complex_blocks((k_ids[:, None] * x_ids[None, :] % length) * unit, 1.0)
        x_back.append(right_table(back.reshape(length, length)))
    return z_fwd, z_back, np.stack(y_fwd), np.stack(y_back), np.stack(x_fwd), np.stack(x_back)


def split_value(value):
    high = value.astype(jnp.bfloat16)
    low = (value - high.astype(jnp.float32)).astype(jnp.bfloat16)
    return high, low


def as_left(value):
    high, low = split_value(value)
    return jnp.concatenate([high, low, high], axis=1)


def as_right_tr(value):
    high, low = split_value(value)
    return jnp.concatenate([high, high, low], axis=1)


def as_right(value):
    high, low = split_value(value)
    return jnp.concatenate([high, high, low], axis=0)


def left_rows(table):
    width = table.shape[1] // 2
    return jnp.concatenate([table, table[:, :width]], axis=1)


def right_rows(table):
    depth = table.shape[0] // 2
    return jnp.concatenate([table[:depth], table], axis=0)


def y_product(table, value):
    high, low = split_value(value)
    both = matmul(jnp.concatenate([table[:, :256], table[:, 256:]], axis=0), high)
    return both[:256] + both[256:] + matmul(table[:, :256], low)


def matmul(left, right):
    return lax.dot_general(
        left, right, (((1,), (0,)), ((), ())), preferred_element_type=jnp.float32
    )


def matmul_tr(left, right):
    return lax.dot_general(
        left, right, (((1,), (1,)), ((), ())), preferred_element_type=jnp.float32
    )


def lane_ids(rows):
    return lax.broadcasted_iota(jnp.int32, (rows, 128), 1)


def z_pieces(spec_hbm, spec_ref, grid_hbm, grid_ref, sems):
    def spec(step, back):
        group, part = step // 2 * 2, pl.multiple_of(step % 2 * 8, 8)
        place = (slice(None), pl.ds(group, 2), pl.ds(part, 8))
        ends = [spec_hbm.at[place], spec_ref.at[step, :, pl.ds(0, 2)]]
        return pltpu.make_async_copy(*(ends[::-1] if back else ends), sems.at[0, step])

    def grid(step, side, back):
        group, part = step // 2 * 2, pl.multiple_of(step % 2 * 16, 16)
        place = (pl.ds(group, 2), slice(None), pl.ds(part, 16))
        ends = [
            grid_hbm.at[place + (pl.ds(side * 128, 128),)],
            grid_ref.at[step, side, :, :, pl.ds(0, 16)],
        ]
        number = (2 if back else 0) + 1 + side
        return pltpu.make_async_copy(*(ends[::-1] if back else ends), sems.at[number, step])

    return spec, grid


def z_forward(table_hbm, phi_hbm, out_hbm, table_ref, phi_ref, out_ref, sems):
    spec, grid = z_pieces(out_hbm, out_ref, phi_hbm, phi_ref, sems)
    steps = groups * 2
    table = pltpu.make_async_copy(table_hbm, table_ref, sems.at[4, 0])
    table.start()
    for step in range(steps):
        for side in range(2):
            grid(step, side, False).start()
    table.wait()
    rows_ref = phi_ref.reshape((steps + 1) * 3072, 128)
    flat_ref = out_ref.reshape((steps + 1) * 3072, 128)

    def body(step, carry):
        for side in range(2):
            grid(step, side, False).wait()
        base = pl.multiple_of(step * 3072, 8)
        for batch in range(4):
            block = jnp.concatenate(
                [
                    jnp.concatenate(
                        [
                            rows_ref[pl.ds(base + side * 1536 + batch * 4 + y, 64, stride=24), :]
                            for side in range(2)
                        ],
                        axis=1,
                    )
                    for y in range(4)
                ],
                axis=0,
            )
            spectrum = matmul_tr(left_rows(table_ref[...]), as_right_tr(block))
            for pair in range(2):
                for part in range(2):
                    start = base + part * 8 + batch * 2 + pair
                    flat_ref[pl.ds(start, 128, stride=24), :] = spectrum[
                        part * 128 : part * 128 + 128, pair * 128 : pair * 128 + 128
                    ]
        spec(step, True).start()
        return carry

    lax.fori_loop(0, steps, body, 0)
    for step in range(steps):
        spec(step, True).wait()


def y_there(in_ref, y_ref, left_ref, ready=lambda: None):
    lanes = lane_ids(256)
    low_half = lanes < 64
    first_bit = lane_ids(128) // 32 % 2 == 0
    halves = []
    for pp in range(2):
        evens, odds = [], []
        for place in (pp, pp + 2):
            first, second = [
                jnp.concatenate(
                    [in_ref[pz * 8 + place * 2 + side].reshape(32, 128) for pz in range(8)], axis=0
                )
                for side in range(2)
            ]
            evens.append(jnp.where(low_half, first, pltpu.roll(second, 64, 1)))
            odds.append(jnp.where(low_half, pltpu.roll(first, 64, 1), second))
        rights = [as_right(jnp.concatenate(pieces, axis=1)) for pieces in (evens, odds)]
        if pp == 0:
            ready()
        even, odd = [matmul(left_rows(y_ref[side]), rights[side]) for side in range(2)]
        low, high = even + odd, even - odd
        halves.append(
            [
                [side[:, :128] + side[:, 128:], side[:, :128] - side[:, 128:]]
                for side in (low, high)
            ]
        )
    for parity in range(2):
        for side in range(2):
            for part in range(2):
                rows = slice(part * 128, part * 128 + 128)
                zero = halves[0][side][parity][rows]
                one = halves[1][side][parity][rows]
                values = (
                    jnp.where(first_bit, zero, pltpu.roll(one, 32, 1)),
                    jnp.where(first_bit, pltpu.roll(zero, 96, 1), one),
                )
                for v, value in enumerate(values):
                    high, low = split_value(value)
                    start = v * 256 + side * 128
                    for place, piece in enumerate((high, low)):
                        column = place * 256 + part * 128
                        left_ref[parity, start : start + 128, column : column + 128] = piece


def x_there(left_ref, x_ref, out_ref):
    for parity in range(2):
        product = matmul(left_rows(left_ref[parity]), right_rows(x_ref[parity]))
        for v in range(2):
            out_ref[v, :, parity * 256 : parity * 256 + 256] = product[v * 256 : v * 256 + 256]


def x_back(in_ref, x_ref, mid_ref):
    products = []
    for parity in range(2):
        columns = slice(parity * 256, parity * 256 + 256)
        block = jnp.concatenate([in_ref[0, :, columns], in_ref[1, :, columns]], axis=0)
        products.append(matmul(as_left(block), right_rows(x_ref[parity])))
    mid_ref[0] = products[0] + products[1]
    mid_ref[1] = products[0] - products[1]


def y_back(mid_ref, y_ref, out_ref):
    lanes = lane_ids(256)
    low_half = lanes < 64
    first_bit = lanes // 32 % 2 == 0
    for side in range(2):
        evens, odds = ([], []), ([], [])
        for part in range(2):
            zero = mid_ref[side, :256, part * 128 : part * 128 + 128]
            one = mid_ref[side, 256:, part * 128 : part * 128 + 128]
            merged = (
                jnp.where(first_bit, zero, pltpu.roll(one, 32, 1)),
                jnp.where(first_bit, pltpu.roll(zero, 96, 1), one),
            )
            for pp in range(2):
                evens[pp].append(merged[pp][:128] + merged[pp][128:])
                odds[pp].append(merged[pp][:128] - merged[pp][128:])
        results = []
        for parity, pieces in enumerate((evens, odds)):
            right = jnp.concatenate([jnp.concatenate(p, axis=0) for p in pieces], axis=1)
            results.append(y_product(y_ref[parity], right))
        for pp in range(2):
            even = results[0][:, pp * 128 : pp * 128 + 128]
            odd = results[1][:, pp * 128 : pp * 128 + 128]
            place = (side * 2 + pp) * 2
            first = jnp.where(low_half, even, pltpu.roll(odd, 64, 1))
            second = jnp.where(low_half, pltpu.roll(even, 64, 1), odd)
            for pz in range(8):
                rows = slice(pz * 32, pz * 32 + 32)
                out_ref[pz * 8 + place] = first[rows].reshape(2, 16, 128)
                out_ref[pz * 8 + place + 1] = second[rows].reshape(2, 16, 128)


def signed_index(indices, length):
    half = length // 2
    return jnp.where(indices >= half, indices - length, indices).astype(jnp.float32)


def waves_x(wave_z, length):
    half = length // 2
    column = lax.broadcasted_iota(jnp.int32, (8, length), 1)
    kx = jnp.where(column >= half, column * 2 - (length - 1), column * 2)
    wx = signed_index(kx, length)
    keep = jnp.where(kx == half, 0.0, 1.0 / float(length * length * length))
    return wx, wx * wx + wave_z * wave_z, keep


def waves_y(row, length):
    ky = lax.broadcasted_iota(jnp.int32, (8, length), 0) + row
    return signed_index(ky, length), jnp.where(ky == length // 2, 0.0, 1.0)


def pick(value, part):
    half = value.shape[1] // 4
    return jnp.concatenate(
        [value[:, c * half : (c + 1) * half] for c in (part, part + 2)], axis=1
    )


def join(real, imag):
    half = real.shape[1] // 2
    pieces = [real[:, :half], imag[:, :half], real[:, half:], imag[:, half:]]
    return jnp.concatenate(pieces, axis=1)


def driving(strain, wx, wy, wz, squared, keep):
    inverse = 1.0 / jnp.maximum(squared, 1.0)
    trace = lame_first * (strain[0] + strain[1] + strain[2])
    s11 = trace + 2.0 * shear_mod * strain[0]
    s22 = trace + 2.0 * shear_mod * strain[1]
    s33 = trace + 2.0 * shear_mod * strain[2]
    s23 = 2.0 * shear_mod * strain[3]
    s13 = 2.0 * shear_mod * strain[4]
    s12 = 2.0 * shear_mod * strain[5]
    t1 = (s11 * wx + s12 * wy + s13 * wz) * inverse
    t2 = (s12 * wx + s22 * wy + s23 * wz) * inverse
    t3 = (s13 * wx + s23 * wy + s33 * wz) * inverse
    normal = (wx * t1 + wy * t2 + wz * t3) * (relax_coef * inverse)
    u1 = t1 - normal * wx
    u2 = t2 - normal * wy
    u3 = t3 - normal * wz
    return [
        keep * (strain[0] - wx * u1),
        keep * (strain[1] - wy * u2),
        keep * (strain[2] - wz * u3),
        keep * (2.0 * strain[3] - (wy * u3 + wz * u2)),
        keep * (2.0 * strain[4] - (wx * u3 + wz * u1)),
        keep * (2.0 * strain[5] - (wx * u2 + wy * u1)),
    ]


def middle(coef_hbm, in_ref, yf_hbm, xf_hbm, xb_hbm, yb_hbm, out_hbm, *scratch):
    yf_ref, xf_ref, xb_ref, yb_ref, coef_ref, field_ref, lefts, mids, out_ref, sems = scratch
    length = field_ref.shape[1]
    steps = groups * 2

    def part_of(ref, step):
        return ref.at[
            pl.ds(step % 2 * 64, 64),
            pl.ds(step // 2 * 2, 2),
        ]

    def departure(step):
        return pltpu.make_async_copy(out_ref.at[step], part_of(out_hbm, step), sems.at[1, step])

    def fields_of(step):
        return field_ref.at[pl.ds(step * 2, 2)]

    moves = [(yf_hbm, yf_ref), (xf_hbm, xf_ref), (xb_hbm, xb_ref), (yb_hbm, yb_ref)]
    moves.append((coef_hbm, coef_ref))
    copies = [
        pltpu.make_async_copy(source, target, sems.at[0, number])
        for number, (source, target) in enumerate(moves)
    ]
    for copy in copies:
        copy.start()

    def there_first(step, slot):
        ready = copies[0].wait if isinstance(step, int) and step == 0 else lambda: None
        y_there(part_of(in_ref, step), yf_ref, lefts[slot], ready)

    def there_second(step, slot):
        x_there(lefts[slot], xf_ref, fields_of(step))

    there_first(0, 0)
    copies[1].wait()

    def there(turn, carry):
        for slot in range(2):
            there_first(turn * 2 + slot + 1, 1 - slot)
            there_second(turn * 2 + slot, slot)
        return carry

    lax.fori_loop(0, groups - 1, there, 0)
    there_first(steps - 1, 1)
    there_second(steps - 2, 0)
    there_second(steps - 1, 1)
    copies[4].wait()
    wave_z = coef_ref[12, 0]
    places = [(p % 6 // 2 * 2 + p // 6) * 2 + p % 2 for p in range(12)]

    wx, squared_xz, keep_x = waves_x(wave_z, length)

    def tile(step, carry):
        row = pl.multiple_of(step * 8, 8)
        rows = pl.ds(row, 8)
        wy, keep_y = waves_y(row, length)
        squared = squared_xz + wy * wy
        keep = keep_x * keep_y
        half_grad = keep * squared * (grad_coef * (two_pi / length) ** 2)
        grad = join(half_grad, half_grad)
        strains = None
        for q, place in enumerate(places):
            value = field_ref[place, rows, :]
            terms = [coef_ref[q, m] * value for m in range(6)]
            strains = terms if q == 0 else [total + term for total, term in zip(strains, terms)]
        parts = [
            driving([pick(total, part) for total in strains], wx, wy, wave_z, squared, keep)
            for part in range(2)
        ]
        drive = [join(parts[0][m], parts[1][m]) for m in range(6)]
        for p, place in enumerate(places):
            total = grad * field_ref[place, rows, :]
            for m in range(6):
                total = total + coef_ref[p, 6 + m] * drive[m]
            field_ref[place, rows, :] = total
        return carry

    lax.fori_loop(0, length // 8, tile, 0, unroll=2)
    copies[2].wait()
    copies[3].wait()

    def back_first(step, slot):
        x_back(fields_of(step), xb_ref, mids[slot])

    def back_second(step, slot):
        y_back(mids[slot], yb_ref, out_ref.at[step])
        departure(step).start()

    back_first(0, 0)

    def back(turn, carry):
        for slot in range(2):
            back_first(turn * 2 + slot + 1, 1 - slot)
            back_second(turn * 2 + slot, slot)
        return carry

    lax.fori_loop(0, groups - 1, back, 0)
    back_first(steps - 1, 1)
    back_second(steps - 2, 0)
    back_second(steps - 1, 1)
    for step in range(steps):
        departure(step).wait()


def squares(phi_ref, out_ref):
    total = phi_ref[0] * phi_ref[0]
    for v in range(1, 2 * groups):
        total = total + phi_ref[v] * phi_ref[v]
    out_ref[...] = total


def local_part(phi_ref, own_ref, partner_ref, out_ref):
    phi = phi_ref[...]
    total_sq = own_ref[...] + partner_ref[...]
    chemical = phi - landau_cubic * phi * phi + landau_quartic * phi * total_sq[None]
    out_ref[...] = phi - mobility * chemical


def z_back(table_hbm, spec_hbm, base_hbm, out_hbm, table_ref, spec_ref, base_ref, sems):
    spec, grid = z_pieces(spec_hbm, spec_ref, base_hbm, base_ref, sems)
    grid_out = z_pieces(spec_hbm, spec_ref, out_hbm, base_ref, sems)[1]
    steps = groups * 2
    table = pltpu.make_async_copy(table_hbm, table_ref, sems.at[5, 0])
    for step in range(steps):
        spec(step, False).start()
        for side in range(2):
            grid(step, side, False).start()
        if step == 0:
            table.start()
    table.wait()
    flat_ref = spec_ref.reshape((steps + 1) * 3072, 128)
    rows_ref = base_ref.reshape((steps + 1) * 3072, 128)

    def body(step, carry):
        base = pl.multiple_of(step * 3072, 8)
        spec(step, False).wait()
        for side in range(2):
            grid(step, side, False).wait()
        for batch in range(4):
            lefts = []
            for pair in range(2):
                turned = []
                for part in range(2):
                    start = base + part * 8 + batch * 2 + pair
                    turned.append(flat_ref[pl.ds(start, 128, stride=24), :].T)
                lefts.append(jnp.concatenate(turned, axis=1))
            force = matmul(as_left(jnp.concatenate(lefts, axis=0)), right_rows(table_ref[...]))
            for y in range(4):
                for side in range(2):
                    rows = pl.ds(base + side * 1536 + batch * 4 + y, 64, stride=24)
                    lanes = slice(side * 128, side * 128 + 128)
                    rows_ref[rows, :] = rows_ref[rows, :] + force[y * 64 : y * 64 + 64, lanes]
        for side in range(2):
            grid_out(step, side, True).start()
        return carry

    lax.fori_loop(0, steps, body, 0)
    for step in range(steps):
        for side in range(2):
            grid_out(step, side, True).wait()


def params(count):
    return pltpu.CompilerParams(
        dimension_semantics=("arbitrary",) * count, vmem_limit_bytes=vmem_bytes
    )


def cost(flops, moved):
    return pl.CostEstimate(flops=int(flops), bytes_accessed=int(moved), transcendentals=0)


def hbm(shape):
    return pltpu.HBM(shape, jnp.float32)


def in_hbm(array):
    return pltpu.with_memory_space_constraint(array, pltpu.HBM)


group_bytes = 2 * 32 * 32 * 256 * 4


def call_z_forward(phi, table):
    return pl.pallas_call(
        z_forward,
        in_specs=[anywhere, anywhere],
        out_specs=anywhere,
        out_shape=hbm((128, 2 * groups, 16, 128)),
        scratch_shapes=[
            pltpu.VMEM(table.shape, jnp.bfloat16),
            pltpu.VMEM((2 * groups + 1, 2, 2, 32, 24, 128), jnp.float32),
            pltpu.VMEM((2 * groups + 1, 128, 3, 8, 128), jnp.float32),
            pltpu.SemaphoreType.DMA((5, 2 * groups)),
        ],
        compiler_params=pltpu.CompilerParams(vmem_limit_bytes=vmem_bytes),
        cost_estimate=cost(2.4e9, 2 * groups * group_bytes),
        name="z_forward",
    )(table, in_hbm(phi))


def call_squares(phi):
    return pl.pallas_call(
        squares,
        grid=(4,),
        in_specs=[pl.BlockSpec((2 * groups, 32, 8, 256), lambda j: (0, 0, j, 0))],
        out_specs=pl.BlockSpec((32, 8, 256), lambda j: (0, j, 0)),
        out_shape=hbm((32, 32, 256)),
        compiler_params=params(1),
        cost_estimate=cost(20e6, groups * group_bytes),
        name="squares",
    )(in_hbm(phi))


def call_local(phi, own, partner):
    return pl.pallas_call(
        local_part,
        grid=(groups, 4),
        in_specs=[
            pl.BlockSpec((2, 32, 8, 256), lambda g, j: (g, 0, j, 0)),
            pl.BlockSpec((32, 8, 256), lambda g, j: (0, j, 0)),
            pl.BlockSpec((32, 8, 256), lambda g, j: (0, j, 0)),
        ],
        out_specs=pl.BlockSpec((2, 32, 8, 256), lambda g, j: (g, 0, j, 0)),
        out_shape=hbm(phi.shape),
        compiler_params=params(2),
        cost_estimate=cost(50e6, 3 * groups * group_bytes),
        name="local_part",
    )(in_hbm(phi), in_hbm(own), partner)


anywhere = pl.BlockSpec(memory_space=pl.ANY)
inside = pl.BlockSpec(memory_space=pltpu.VMEM)


def call_middle(coefs, spec, tables):
    shapes = [
        *[pltpu.VMEM(table.shape, jnp.bfloat16) for table in tables],
        pltpu.SMEM(coefs.shape, jnp.float32),
        pltpu.VMEM((4 * groups, 256, 512), jnp.float32),
        [pltpu.VMEM((2, 512, 512), jnp.bfloat16)] * 2,
        [pltpu.VMEM((2, 512, 256), jnp.float32)] * 2,
        pltpu.VMEM((2 * groups, 64, 2, 16, 128), jnp.float32),
        pltpu.SemaphoreType.DMA((2, 2 * groups)),
    ]
    return pl.pallas_call(
        middle,
        in_specs=[anywhere, inside] + [anywhere] * len(tables),
        out_specs=anywhere,
        out_shape=hbm(spec.shape),
        scratch_shapes=shapes,
        compiler_params=pltpu.CompilerParams(vmem_limit_bytes=vmem_bytes),
        cost_estimate=cost(20e9, 6 * groups * group_bytes),
        name="middle",
    )(coefs, pltpu.with_memory_space_constraint(spec, pltpu.VMEM), *tables)


def call_z_back(spec, base, table):
    return pl.pallas_call(
        z_back,
        in_specs=[anywhere, anywhere, anywhere],
        out_specs=anywhere,
        out_shape=hbm(base.shape),
        scratch_shapes=[
            pltpu.VMEM(table.shape, jnp.bfloat16),
            pltpu.VMEM((2 * groups + 1, 128, 3, 8, 128), jnp.float32),
            pltpu.VMEM((2 * groups + 1, 2, 2, 32, 24, 128), jnp.float32),
            pltpu.SemaphoreType.DMA((6, 2 * groups)),
        ],
        compiler_params=pltpu.CompilerParams(vmem_limit_bytes=vmem_bytes),
        cost_estimate=cost(2.4e9, 3 * groups * group_bytes),
        name="z_back",
    )(table, spec, in_hbm(base))


def exchange(block):
    return lax.all_to_all(block, every, split_axis=0, concat_axis=0, tiled=True)


def coefficients(strains, variant_strain, variants):
    bank_rows = strains.shape[0]
    picked = variant_strain[:variants]
    one_hot = (picked[:, None] == jnp.arange(bank_rows, dtype=jnp.int32)[None, :]).astype(
        jnp.float32
    )
    chosen = jnp.dot(one_hot, strains, precision=highest)
    trace = lame_first * (chosen[:, 0] + chosen[:, 1] + chosen[:, 2])
    diagonal = jnp.asarray([1.0, 1.0, 1.0, 0.0, 0.0, 0.0], jnp.float32)
    stress = trace[:, None] * diagonal[None, :] + 2.0 * shear_mod * chosen
    plane = lax.axis_index(every).astype(jnp.float32)
    last = jnp.full((1, 12), plane, jnp.float32)
    return jnp.concatenate([jnp.concatenate([chosen, stress], axis=1), last], axis=0)


def shards(order_field, strains, variant_strain):
    length = order_field.shape[3]
    tables = [in_hbm(jnp.asarray(table)) for table in dft_tables(length)]
    z_fwd, z_inv, y_fwd, y_inv, x_fwd, x_inv = tables
    coefs = coefficients(strains, variant_strain, 12)
    sent, later_field = lax.optimization_barrier((call_z_forward(order_field, z_fwd), order_field))
    arrived = exchange(sent)
    own = call_squares(later_field)
    own, arrived = lax.optimization_barrier((own, arrived))
    partner = lax.ppermute(own, "var", [(0, 1), (1, 0)])
    sent = call_middle(coefs, arrived, (y_fwd, x_fwd, x_inv, y_inv))
    sent, partner = lax.optimization_barrier((sent, partner))
    returned = exchange(sent)
    base = call_local(order_field, own, partner)
    return call_z_back(returned, base, z_inv)


def solution(mesh):
    placed = (P("var", "py", "pz", None), P(), P())
    return jax.shard_map(
        shards, mesh=mesh, in_specs=placed, out_specs=P("var", "py", "pz", None), check_vma=False
    )
```
